128 devices in a mesh: row: 32 (over z, y, core), ch: 4 (over x).
Axes of the slice: x: 4, y: 4, z: 4, core: 2. Of those that a mesh axis runs over, the one named last changes fastest.
Arguments:
- pair: float32 [512, 512, 128], P('row'), may hold values from -6 to 6
- mask: int32 [512], replicated, may hold values 0 or 1
- in_gain: float32 [2, 128], replicated, may hold values from 0.1 to 1.9
- in_bias: float32 [2, 128], replicated, may hold values from -3 to 3
- w_proj: bfloat16 [2, 128, 4, 128], P(None, None, None, 'ch'), may hold values from -0.5 to 0.5
- w_gate: bfloat16 [2, 128, 128], replicated, may hold values from -0.5 to 0.5
- out_gain: float32 [2, 128], P(None, 'ch'), may hold values from 0.1 to 1.9
- out_bias: float32 [2, 128], P(None, 'ch'), may hold values from -3 to 3
- w_out: bfloat16 [2, 128, 128], P(None, 'ch'), may hold values from -0.5 to 0.5
Outputs:
- updated: float32 [512, 512, 128], P('row')
The draws below stay inside these ranges and needn't reach their ends.
All inputs are finite; a program needn't handle non-finite values.
Results may differ from the reference program's by a relative error of at most 0.009.
Values may be sent and summed in bfloat16 or wider, within the bound.
No kernel may reach another device: no remote copies, remote signals or barrier semaphores. Data moves between devices by JAX's collectives and lax.ppermute only.
A program may use at most 192 MiB of HBM per device.

```python
import jax
import jax.numpy as jnp
from jax import lax

C = 128
HID = 128
N = 512


def plant(array, stream_key, least, top_value):
    index_at = [jax.random.randint(jax.random.fold_in(stream_key, axis), (), 0, length) for axis, length in enumerate(array.shape)]
    longest = array.shape.index(max(array.shape))
    beside = index_at[:longest] + [(index_at[longest] + 1) % array.shape[longest]] + index_at[longest + 1:]
    return array.at[tuple(index_at)].set(least).at[tuple(beside)].set(top_value)


def block_scale(key, shape, split, low, top_value):
    level, own = 1.0, jax.random.fold_in(key, 6)
    for dim, parts in split:
        draws = jnp.exp(jax.random.uniform(jax.random.fold_in(own, dim), (parts,), jnp.float32, low / len(split), top_value / len(split)))
        level = level * jnp.repeat(draws, shape[dim] // parts).reshape([-1 if axis == dim else 1 for axis in range(len(shape))])
    return level


def scatter_about(stream_key, extent, spread, reach, shards=(), held_as=jnp.bfloat16):
    values = jax.random.normal(stream_key, extent, jnp.float32) * spread
    if len(shards) > 0:
        values = block_scale(stream_key, extent, shards, -0.22, 0.18) * values
    return jnp.clip(values, min=-reach, max=reach).astype(held_as)


def setup_inputs(seed: int = 0) -> dict:
    arg_keys = jax.random.split(jax.random.key(seed), 10)
    pair = scatter_about(arg_keys[0], (N, N, C), 1.0, 6.0, ((0, 32),), jnp.float32)
    mask = plant((jax.random.randint(arg_keys[1], (N,), 0, 8) < 7).astype(jnp.int32), jax.random.fold_in(arg_keys[1], 1), 0, 1)
    in_gain = jnp.clip(1.0 + 0.18 * jax.random.normal(arg_keys[2], (2, C), jnp.float32), 0.1, 1.9)
    in_bias = scatter_about(arg_keys[3], (2, C), 0.5, 3.0, (), jnp.float32)
    w_proj = scatter_about(arg_keys[4], (2, C, 4, HID), C ** -0.5, 0.5, ((3, 4),))
    w_gate = scatter_about(arg_keys[5], (2, C, C), C ** -0.5, 0.5)
    out_gain = jnp.clip(1.0 + 0.18 * jax.random.normal(arg_keys[6], (2, HID), jnp.float32), 0.1, 1.9)
    out_bias = scatter_about(arg_keys[7], (2, HID), 0.5, 3.0, ((1, 4),), jnp.float32)
    w_out = scatter_about(arg_keys[8], (2, HID, C), HID ** -0.5, 0.5, ((1, 4),))
    return dict(pair=pair, mask=mask, in_gain=in_gain, in_bias=in_bias, w_proj=w_proj, w_gate=w_gate, out_gain=out_gain, out_bias=out_bias, w_out=w_out)


def layer_norm(values, gain, bias):
    mean = lax.optimization_barrier(jnp.mean(values, -1, keepdims=True))
    var = lax.optimization_barrier(jnp.mean(jnp.square(values - mean), -1, keepdims=True))
    return (values - mean) * lax.rsqrt(var + 1e-05) * gain + bias

def reference(pair, mask, in_gain, in_bias, w_proj, w_gate, out_gain, out_bias, w_out):
    mask_f = mask.astype(jnp.float32)
    pair_mask = (mask_f[:, None] * mask_f[None, :])[:, :, None]
    state = pair
    for layer in range(2):
        normed = layer_norm(state, in_gain[layer], in_bias[layer]).astype(jnp.bfloat16)
        flat = normed.reshape(N * N, C)
        proj = jnp.dot(flat, w_proj[layer].reshape(C, 4 * HID), preferred_element_type=jnp.float32)
        proj = proj.reshape(N, N, 4, HID)
        left = (jax.nn.sigmoid(proj[:, :, 0]) * proj[:, :, 1] * pair_mask).astype(jnp.bfloat16)
        right = (jax.nn.sigmoid(proj[:, :, 2]) * proj[:, :, 3] * pair_mask).astype(jnp.bfloat16)
        left_f = left.astype(jnp.float32)
        right_f = right.astype(jnp.float32)
        if layer == 0:
            mixed = jnp.einsum('ikc,jkc->ijc', left_f, right_f, precision=lax.Precision.HIGHEST)
        else:
            mixed = jnp.einsum('kic,kjc->ijc', left_f, right_f, precision=lax.Precision.HIGHEST)
        hidden = layer_norm(mixed, out_gain[layer], out_bias[layer]).astype(jnp.bfloat16)
        change = jnp.dot(hidden.reshape(N * N, HID), w_out[layer], preferred_element_type=jnp.float32)
        gate = jax.nn.sigmoid(jnp.dot(flat, w_gate[layer], preferred_element_type=jnp.float32))
        state = state + (gate * change).reshape(N, N, C)
    return state
```

```python
import functools

import jax
import jax.numpy as jnp
from jax import lax
from jax.experimental import pallas as pl
from jax.experimental.pallas import tpu as pltpu
from jax.sharding import PartitionSpec as P

F32, BF16 = jnp.float32, jnp.bfloat16
N, C, T = 512, 128, 128
RB = 16
G, R = 4, 32
D = C // G
VMEM_LIMIT = 32 * 1024 * 1024

PK_PROJ, PK_OUT, PK_NORM, PK = 0, 128, 192, 224


def dot(a, b, ca=1, cb=0):
    return lax.dot_general(a, b, (((ca,), (cb,)), ((), ())), preferred_element_type=F32)


def column(row):
    return jnp.broadcast_to(row, (C, C)).T


def norm_cols(v, gain, bias):
    mean = jnp.mean(v, 0, keepdims=True)
    cent = v - mean
    var = jnp.mean(cent * cent, 0, keepdims=True)
    return cent * lax.rsqrt(var + 1e-05) * gain + bias


def sigmoid(v):
    return 0.5 * jnp.tanh(0.5 * v) + 0.5


def gated(gate, value, half_mask):
    return (jnp.tanh(0.5 * gate) + 1.0) * (value * half_mask)


def project0_kernel(ids, mask_s, pair, mask_v, in_gain, in_bias, w, out, left_s, right_s):
    gain, bias = column(in_gain[0:1, :]), column(in_bias[0:1, :])
    cols = mask_v[...] * 0.5
    row0 = ids[0] * RB
    for i in range(RB):
        zn = norm_cols(pair[i].T, gain, bias).astype(BF16)
        proj = dot(w[...], zn)
        half = cols * mask_s[row0 + i].astype(F32)
        left_s[pl.ds(i, D, stride=RB), :] = gated(proj[0:D], proj[D : 2 * D], half)
        right_s[pl.ds(i, D, stride=RB), :] = gated(proj[2 * D : 3 * D], proj[3 * D :], half)
    out[:, 0] = left_s[...].reshape(D, RB, T).astype(BF16)
    out[:, 1] = right_s[...].reshape(D, RB, T).astype(BF16)


def outgoing_kernel(a, out):
    left = a[:, 0].reshape(N, N)
    for h in range(G):
        right = a[8 * h : 8 * h + 8, 1].reshape(T, N)
        out[h] = dot(left, right, 1, 1).reshape(R, RB, T).astype(BF16)


def incoming_kernel(b, out):
    left = jnp.concatenate([b[R * h : R * h + R, 0].reshape(N, T) for h in range(G)], 1)
    for h in range(G):
        right = b[R * h : R * h + R, 1].reshape(N, T)
        out[h] = dot(left, right, 0, 0).reshape(R, RB, T).astype(BF16)


def norm_params(pk, layer):
    parts = jnp.concatenate([pk[g, PK_NORM : PK_NORM + D] for g in range(G)], 0).astype(F32)
    k = 2 * layer
    cols = [parts[:, k + j : k + j + 1] + parts[:, 4 + k + j : 5 + k + j] + parts[:, 8 + k + j : 9 + k + j] for j in (0, 1)]
    w_out = jnp.concatenate(
        [pk[g, PK_OUT + D * layer : PK_OUT + D * (layer + 1)] for g in range(G)], 0
    )
    return cols[0], cols[1], w_out.astype(F32).T.astype(BF16)


def middle_kernel(
    ids, mask_s, y, pair, mask_v, in_gain, in_bias, w_gate, pk, state, normed, out, ys, left_s, right_s
):
    gain0, bias0 = column(in_gain[0:1, :]), column(in_bias[0:1, :])
    gain1, bias1 = column(in_gain[1:2, :]), column(in_bias[1:2, :])
    og, ob, w_out = norm_params(pk, 0)
    og, ob = jnp.broadcast_to(og, (C, T)), jnp.broadcast_to(ob, (C, T))
    w_g = w_gate[0].astype(F32).T.astype(BF16)
    cols = mask_v[...] * 0.5
    row0 = ids[0] * RB
    ys[...] = y[...].astype(F32).reshape(C * RB, T)
    for i in range(RB):
        hidden = norm_cols(ys[pl.ds(i, C, stride=RB), :], og, ob).astype(BF16)
        z = pair[i].T
        gate = sigmoid(dot(w_g, norm_cols(z, gain0, bias0).astype(BF16)))
        z = z + gate * dot(w_out, hidden)
        state[i] = z
        zn = norm_cols(z, gain1, bias1).astype(BF16)
        normed[i] = zn
        half = cols * mask_s[row0 + i].astype(F32)
        for g in range(G):
            proj = dot(pk[g, PK_PROJ : PK_PROJ + C], zn)
            at = pl.ds(i + g * D * RB, D, stride=RB)
            left_s[at, :] = gated(proj[0:D], proj[D : 2 * D], half)
            right_s[at, :] = gated(proj[2 * D : 3 * D], proj[3 * D :], half)
    out[:, 0] = left_s[...].reshape(C, RB, T).astype(BF16)
    out[:, 1] = right_s[...].reshape(C, RB, T).astype(BF16)


def last_kernel(y, state, normed, w_gate, pk, out, ys):
    og, ob, w_out = norm_params(pk, 1)
    og, ob = jnp.broadcast_to(og, (C, T)), jnp.broadcast_to(ob, (C, T))
    w_g = w_gate[1].astype(F32).T.astype(BF16)
    ys[...] = y[...].astype(F32).reshape(C * RB, T)
    for i in range(RB):
        hidden = norm_cols(ys[pl.ds(i, C, stride=RB), :], og, ob).astype(BF16)
        gate = sigmoid(dot(w_g, normed[i]))
        z = state[i] + gate * dot(w_out, hidden)
        out[i] = z.T.astype(BF16)


def spread_kernel(ids, own, up0, up1, down0, down1, far0, far1, out):
    step = pl.program_id(0)

    @pl.when(step == 0)
    def _():
        out[...] = own[...].astype(F32)

    @pl.when(step == 1)
    def _():
        out[0:8] = down0[...].astype(F32)
        out[8:16] = down1[...].astype(F32)

    @pl.when(step == 2)
    def _():
        out[0:8] = far0[...].astype(F32)
        out[8:16] = far1[...].astype(F32)

    @pl.when(step == 3)
    def _():
        out[0:8] = up0[...].astype(F32)
        out[8:16] = up1[...].astype(F32)


def params(**kw):
    return pltpu.CompilerParams(vmem_limit_bytes=VMEM_LIMIT, **kw)


def whole(shape):
    return pl.BlockSpec(shape, lambda *_: (0,) * len(shape))


def on_device(pair, mask, in_gain, in_bias, w_proj, w_gate, out_gain, out_bias, w_out):
    ids = jnp.stack([lax.axis_index("row"), lax.axis_index("ch")]).astype(jnp.int32)
    mask_v = mask.astype(F32)[None]
    w_t = jnp.transpose(w_proj, (0, 2, 3, 1)).reshape(2, 4 * D, C)

    nrm = jnp.stack([out_gain[0], out_bias[0], out_gain[1], out_bias[1]], 1)
    hi = nrm.astype(BF16)
    mid = (nrm - hi.astype(F32)).astype(BF16)
    low = (nrm - hi.astype(F32) - mid.astype(F32)).astype(BF16)
    nrm = jnp.pad(jnp.concatenate([hi, mid, low], 1), ((0, 0), (0, C - 12)))
    own = jnp.concatenate([w_t[1], w_out.reshape(2 * D, C), nrm], 0)
    pk = lax.all_gather(own, "ch", axis=0)

    a = pl.pallas_call(
        project0_kernel,
        out_shape=jax.ShapeDtypeStruct((D, 2, RB, N), BF16),
        grid_spec=pltpu.PrefetchScalarGridSpec(
            num_scalar_prefetch=2,
            grid=(G,),
            in_specs=[
                pl.BlockSpec((RB, T, C), lambda j, *_: (0, j, 0)),
                pl.BlockSpec((1, T), lambda j, *_: (0, j)),
                whole((2, C)),
                whole((2, C)),
                whole((4 * D, C)),
            ],
            out_specs=pl.BlockSpec((D, 2, RB, T), lambda j, *_: (0, 0, 0, j)),
            scratch_shapes=[pltpu.VMEM((D * RB, T), F32)] * 2,
        ),
        compiler_params=params(),
        name="project0",
    )(ids, mask, pair, mask_v, in_gain, in_bias, w_t[0])
    a = lax.all_to_all(a, "row", 0, 0)
    x = pl.pallas_call(
        outgoing_kernel,
        out_shape=jax.ShapeDtypeStruct((G, R, RB, T), BF16),
        compiler_params=params(),
        name="outgoing",
    )(a)
    y = lax.all_to_all(x.reshape(G * R, RB, T), ("ch", "row"), 0, 0)
    state, normed, b = pl.pallas_call(
        middle_kernel,
        out_shape=(
            jax.ShapeDtypeStruct((RB, C, T), F32),
            jax.ShapeDtypeStruct((RB, C, T), BF16),
            jax.ShapeDtypeStruct((C, 2, RB, T), BF16),
        ),
        grid_spec=pltpu.PrefetchScalarGridSpec(
            num_scalar_prefetch=2,
            grid=(1,),
            in_specs=[
                whole((C, RB, T)),
                pl.BlockSpec((RB, T, C), lambda j, ids, _: (0, ids[1], 0)),
                pl.BlockSpec((1, T), lambda j, ids, _: (0, ids[1])),
                whole((2, C)),
                whole((2, C)),
                whole((2, C, C)),
                whole((G, PK, C)),
            ],
            out_specs=(whole((RB, C, T)), whole((RB, C, T)), whole((C, 2, RB, T))),
            scratch_shapes=[pltpu.VMEM((C * RB, T), F32)] * 3,
        ),
        compiler_params=params(),
        name="middle",
    )(ids, mask, y, pair, mask_v, in_gain, in_bias, w_gate, pk)
    b = lax.all_to_all(b, ("ch", "row"), 0, 0)
    x = pl.pallas_call(
        incoming_kernel,
        out_shape=jax.ShapeDtypeStruct((G, R, RB, T), BF16),
        compiler_params=params(),
        name="incoming",
    )(b)
    y = lax.all_to_all(x.reshape(G * R, RB, T), ("ch", "row"), 0, 0)
    z = pl.pallas_call(
        last_kernel,
        out_shape=jax.ShapeDtypeStruct((RB, T, C), BF16),
        scratch_shapes=[pltpu.VMEM((C * RB, T), F32)],
        compiler_params=params(),
        name="last",
    )(y, state, normed, w_gate, pk)

    up = functools.partial(lax.ppermute, axis_name="ch", perm=[(k, (k + 1) % G) for k in range(G)])
    down = functools.partial(lax.ppermute, axis_name="ch", perm=[(k, (k - 1) % G) for k in range(G)])
    z0, z1 = z[:8], z[8:]
    up0, down1 = up(z0), down(z1)
    up1, down0 = up(z1), down(z0)
    far0, far1 = up(up0), down(down1)
    half = whole((RB // 2, T, C))
    return pl.pallas_call(
        spread_kernel,
        out_shape=jax.ShapeDtypeStruct((RB, N, C), F32),
        grid_spec=pltpu.PrefetchScalarGridSpec(
            num_scalar_prefetch=1,
            grid=(G,),
            in_specs=[whole((RB, T, C))] + [half] * 6,
            out_specs=pl.BlockSpec((RB, T, C), lambda s, ids: (0, lax.rem(ids[1] + s, G), 0)),
        ),
        compiler_params=params(),
        name="spread",
    )(ids, z, up0, up1, down0, down1, far0, far1)


def solution(mesh):
    placed = (
        P("row", None, None),
        P(),
        P(),
        P(),
        P(None, None, None, "ch"),
        P(),
        P(None, "ch"),
        P(None, "ch"),
        P(None, "ch", None),
    )
    return jax.shard_map(
        on_device, mesh=mesh, in_specs=placed, out_specs=P("row", None, None), check_vma=False
    )
```

```python
import functools

import jax
import jax.numpy as jnp
from jax import lax
from jax.experimental import pallas as pl
from jax.experimental.pallas import tpu as pltpu
from jax.sharding import PartitionSpec as P

F32, BF16 = jnp.float32, jnp.bfloat16
N, C, T = 512, 128, 128
RB = 16
G, R = 4, 32
D = C // G
HB = RB // 2
HBM, VMEM = pltpu.HBM, pltpu.VMEM
VMEM_LIMIT = 32 * 1024 * 1024
WHOLE_VMEM = 60 * 1024 * 1024
MOST_VMEM = 51 * 1024 * 1024

PK_PROJ, PK_OUT, PK_NORM, PK = 0, 128, 192, 208


def dot(a, b, ca=1, cb=0):
    return lax.dot_general(a, b, (((ca,), (cb,)), ((), ())), preferred_element_type=F32)


def column(row):
    return jnp.broadcast_to(row, (C, C)).T


def norm_cols(v, gain, bias):
    mean = jnp.mean(v, 0, keepdims=True)
    cent = v - mean
    var = jnp.mean(cent * cent, 0, keepdims=True)
    return cent * lax.rsqrt(var + 1e-05) * gain + bias


def sigmoid(v):
    return 0.5 * jnp.tanh(0.5 * v) + 0.5


def gated(gate, value, half_mask):
    return (jnp.tanh(0.5 * gate) + 1.0) * (value * half_mask)


def project0_kernel(
    pair, mask, in_gain, in_bias, w, w_out, out_gain, out_bias, out, own,
    rows, mask_v, mask_s, gb, w_v, wo_v, og_v, left_s, right_s, sems,
):
    small = [
        (mask, mask_v),
        (mask, mask_s),
        (in_gain, gb.at[0]),
        (in_bias, gb.at[1]),
        (w, w_v),
        (w_out, wo_v),
        (out_gain, og_v.at[0]),
        (out_bias, og_v.at[1]),
    ]
    big = [(pair.at[i], rows.at[i]) for i in range(RB)]
    copies = [pltpu.make_async_copy(*ends, sems.at[k]) for k, ends in enumerate(small + big)]
    few = len(small)
    for copy in copies[few : few + 2] + copies[:few] + copies[few + 2 :]:
        copy.start()
    for copy in copies[:few]:
        copy.wait()
    gain, bias = column(gb[0, 0:1, :]), column(gb[1, 0:1, :])
    cols = mask_v[...].astype(F32) * 0.5
    row0 = lax.axis_index("row") * RB
    for i in range(RB):
        copies[few + i].wait()
        zn = jnp.concatenate(
            [norm_cols(rows[i, T * h : T * h + T].T, gain, bias).astype(BF16) for h in range(G)], 1
        )
        proj = dot(w_v[0], zn)
        half = cols * mask_s[0, row0 + i].astype(F32)
        left = gated(proj[0:D], proj[D : 2 * D], half)
        right = gated(proj[2 * D : 3 * D], proj[3 * D :], half)
        for h in range(G):
            left_s[h, pl.ds(i, D, stride=RB), :] = left[:, T * h : T * h + T]
            right_s[h, pl.ds(i, D, stride=RB), :] = right[:, T * h : T * h + T]
    for h in range(G):
        out[:, 0, :, T * h : T * h + T] = left_s[h].reshape(D, RB, T).astype(BF16)
        out[:, 1, :, T * h : T * h + T] = right_s[h].reshape(D, RB, T).astype(BF16)

    own[:PK_OUT] = w_v[1]
    own[PK_OUT:PK_NORM] = wo_v[...].reshape(2 * D, C)
    norms = jnp.concatenate([og_v[0], og_v[1]], 0)
    hi = norms.astype(BF16).astype(F32)
    mid = (norms - hi).astype(BF16).astype(F32)
    low = norms - hi - mid
    tile = jnp.concatenate([hi, mid, low, jnp.zeros_like(hi)], 0)
    own[PK_NORM:] = jnp.concatenate([tile, jnp.zeros((16, C - D), F32)], 1).astype(BF16)


def gate0_kernel(pair, in_gain, in_bias, w_gate, state, gate, block, sem):
    at = pl.multiple_of(lax.axis_index("ch") * T, T)
    copy = pltpu.make_async_copy(pair.at[:, pl.ds(at, T), :], block, sem)
    copy.start()
    gain, bias = column(in_gain[0:1, :]), column(in_bias[0:1, :])
    w_g = w_gate[0].astype(F32).T.astype(BF16)
    copy.wait()
    for i in range(RB):
        z = block[i].T
        state[i] = z
        gate[i] = sigmoid(dot(w_g, norm_cols(z, gain, bias).astype(BF16)))


def weights_kernel(own, up, down, far, w_proj, w_out, norms, pk):
    g = lax.axis_index("ch")
    pk[g] = own[...]
    pk[lax.rem(g + 3, G)] = up[...]
    pk[lax.rem(g + 1, G)] = down[...]
    pk[lax.rem(g + 2, G)] = far[...]
    for k in range(G):
        w_proj[k] = pk[k, PK_PROJ : PK_PROJ + C]
    for k in range(G):
        parts = pk[k, PK_NORM:].astype(F32)
        parts = parts[0:4] + parts[4:8] + parts[8:12]
        for j in range(4):
            norms[j, D * k : D * k + D] = column(parts[j : j + 1])[:D]
    for layer in range(2):
        rows = jnp.concatenate(
            [pk[k, PK_OUT + D * layer : PK_OUT + D * (layer + 1)] for k in range(G)], 0
        )
        w_out[layer] = rows.astype(F32).T.astype(BF16)


def outgoing_kernel(a, out):
    left = a[:, 0].reshape(N, N)
    for h in range(G):
        right = a[8 * h : 8 * h + 8, 1].reshape(T, N)
        out[h] = dot(left, right, 1, 1).reshape(R, RB, T).astype(BF16)


def incoming_kernel(b, out):
    left = jnp.concatenate([b[R * h : R * h + R, 0].reshape(N, T) for h in range(G)], 1)
    for h in range(G):
        right = b[R * h : R * h + R, 1].reshape(N, T)
        out[h] = dot(left, right, 0, 0).reshape(R, RB, T).astype(BF16)


def middle_kernel(
    y, z0, gate, mask, in_gain, in_bias, w_proj, w_out, norms, state, normed, out, mask_v, mask_s, ys, left_s, right_s, sems
):
    at = pl.multiple_of(lax.axis_index("ch") * T, T)
    copies = [
        pltpu.make_async_copy(mask.at[:, pl.ds(at, T)], mask_v, sems.at[0]),
        pltpu.make_async_copy(mask, mask_s, sems.at[1]),
    ]
    for copy in copies:
        copy.start()
    gain1, bias1 = column(in_gain[1:2, :]), column(in_bias[1:2, :])
    row0 = lax.axis_index("row") * RB
    ys[...] = y[...].astype(F32).reshape(C * RB, T)
    for copy in copies:
        copy.wait()
    cols = mask_v[...].astype(F32) * 0.5
    for i in range(RB):
        hidden = norm_cols(ys[pl.ds(i, C, stride=RB), :], norms[0], norms[2]).astype(BF16)
        z = z0[i] + gate[i] * dot(w_out[0], hidden)
        state[i] = z
        zn = norm_cols(z, gain1, bias1).astype(BF16)
        normed[i] = zn
        half = cols * mask_s[0, row0 + i].astype(F32)
        for g in range(G):
            proj = dot(w_proj[g], zn)
            rows = pl.ds(i + g * D * RB, D, stride=RB)
            left_s[rows, :] = gated(proj[0:D], proj[D : 2 * D], half)
            right_s[rows, :] = gated(proj[2 * D : 3 * D], proj[3 * D :], half)
    out[:, 0] = left_s[...].reshape(C, RB, T).astype(BF16)
    out[:, 1] = right_s[...].reshape(C, RB, T).astype(BF16)


def last_kernel(y, state, normed, w_gate, w_out, norms, out0, out1, ys):
    w_g = w_gate[1].astype(F32).T.astype(BF16)
    ys[...] = y[...].astype(F32).reshape(C * RB, T)
    for i in range(RB):
        hidden = norm_cols(ys[pl.ds(i, C, stride=RB), :], norms[1], norms[3]).astype(BF16)
        gate = sigmoid(dot(w_g, normed[i]))
        z = state[i] + gate * dot(w_out[1], hidden)
        out = (out0, out1)[i // HB]
        out[i % HB] = z.T.astype(BF16)


def spread_near_kernel(own0, own1, up0, up1, down0, down1, out, buf, sems):
    g = lax.axis_index("ch")
    copies = []
    for k, (shift, lo, hi) in enumerate([(0, own0, own1), (3, up0, up1), (1, down0, down1)]):
        buf[k, :HB] = lo[...].astype(F32)
        buf[k, HB:] = hi[...].astype(F32)
        at = pl.multiple_of(lax.rem(g + shift, G) * T, T)
        copies.append(pltpu.make_async_copy(buf.at[k], out.at[:, pl.ds(at, T), :], sems.at[k]))
        copies[-1].start()
    for copy in copies:
        copy.wait()


def spread_far_kernel(far0, far1, _, out, buf, sems):
    at = pl.multiple_of(lax.rem(lax.axis_index("ch") + 2, G) * T, T)
    copies = []
    for k, far in enumerate((far0, far1)):
        buf[k] = far[...].astype(F32)
        copies.append(
            pltpu.make_async_copy(buf.at[k], out.at[pl.ds(k * HB, HB), pl.ds(at, T), :], sems.at[k])
        )
        copies[-1].start()
    for copy in copies:
        copy.wait()


def params(limit=VMEM_LIMIT):
    return pltpu.CompilerParams(vmem_limit_bytes=limit)


def call(kernel, name, outs, scratch, ins, limit=VMEM_LIMIT):
    return pl.pallas_call(
        kernel,
        out_shape=outs,
        in_specs=[pl.BlockSpec(memory_space=space) for _, space in ins],
        out_specs=jax.tree.map(lambda _: pl.BlockSpec(memory_space=VMEM), outs),
        scratch_shapes=scratch,
        compiler_params=params(limit),
        name=name,
    )(*[value for value, _ in ins])


def on_device(pair, mask, in_gain, in_bias, w_proj, w_gate, out_gain, out_bias, w_out):
    arr = jax.ShapeDtypeStruct
    mask = mask[None]
    w_t = jnp.transpose(w_proj, (0, 2, 3, 1)).reshape(2, 4 * D, C)
    dma = pltpu.SemaphoreType.DMA

    a, own = call(
        project0_kernel,
        "project0",
        (arr((D, 2, RB, N), BF16), arr((PK, C), BF16)),
        [
            pltpu.VMEM((RB, N, C), F32),
            pltpu.VMEM((1, N), jnp.int32),
            pltpu.SMEM((1, N), jnp.int32),
            pltpu.VMEM((2, 2, C), F32),
            pltpu.VMEM((2, 4 * D, C), BF16),
            pltpu.VMEM((2, D, C), BF16),
            pltpu.VMEM((2, 2, D), F32),
            pltpu.VMEM((G, D * RB, T), F32),
            pltpu.VMEM((G, D * RB, T), F32),
            dma((8 + RB,)),
        ],
        [(v, HBM) for v in (pair, mask, in_gain, in_bias, w_t, w_out, out_gain, out_bias)],
        WHOLE_VMEM,
    )

    up = functools.partial(lax.ppermute, axis_name="ch", perm=[(k, (k + 1) % G) for k in range(G)])
    down = functools.partial(lax.ppermute, axis_name="ch", perm=[(k, (k - 1) % G) for k in range(G)])
    cross = functools.partial(lax.ppermute, axis_name="ch", perm=[(k, (k + 2) % G) for k in range(G)])

    a = lax.all_to_all(a, "row", 0, 0)
    w_proj1, w_out_t, norms = call(
        weights_kernel,
        "weights",
        (arr((G, C, C), BF16), arr((2, C, C), BF16), arr((4, C, T), F32)),
        [pltpu.VMEM((G, PK, C), BF16)],
        [(v, VMEM) for v in (own, up(own), down(own), cross(own))],
    )
    state, gate = call(
        gate0_kernel,
        "gate0",
        (arr((RB, C, T), F32), arr((RB, C, T), F32)),
        [pltpu.VMEM((RB, T, C), F32), dma],
        [(pair, HBM), (in_gain, VMEM), (in_bias, VMEM), (w_gate, VMEM)],
        MOST_VMEM,
    )
    a, state, gate, w_proj1, w_out_t, norms = lax.optimization_barrier(
        (a, state, gate, w_proj1, w_out_t, norms)
    )
    x = call(outgoing_kernel, "outgoing", arr((G, R, RB, T), BF16), [], [(a, VMEM)])
    y = lax.all_to_all(x.reshape(G * R, RB, T), ("ch", "row"), 0, 0)
    state, normed, b = call(
        middle_kernel,
        "middle",
        (arr((RB, C, T), F32), arr((RB, C, T), BF16), arr((C, 2, RB, T), BF16)),
        [pltpu.VMEM((1, T), jnp.int32), pltpu.SMEM((1, N), jnp.int32)]
        + [pltpu.VMEM((C * RB, T), F32)] * 3
        + [dma((2,))],
        [(y, VMEM), (state, VMEM), (gate, VMEM), (mask, HBM)]
        + [(v, VMEM) for v in (in_gain, in_bias, w_proj1, w_out_t, norms)],
    )
    b = lax.all_to_all(b, ("ch", "row"), 0, 0)
    x = call(incoming_kernel, "incoming", arr((G, R, RB, T), BF16), [], [(b, VMEM)])
    y = lax.all_to_all(x.reshape(G * R, RB, T), ("ch", "row"), 0, 0)
    half = arr((HB, T, C), BF16)
    z0, z1 = call(
        last_kernel,
        "last",
        (half, half),
        [pltpu.VMEM((C * RB, T), F32)],
        [(v, VMEM) for v in (y, state, normed, w_gate, w_out_t, norms)],
    )
    up0, down1 = up(z0), down(z1)
    up1, down0 = up(z1), down(z0)
    far0, far1 = up(up0), down(down1)
    whole = arr((RB, N, C), F32)
    near = pl.pallas_call(
        spread_near_kernel,
        out_shape=whole,
        in_specs=[pl.BlockSpec(memory_space=VMEM)] * 6,
        out_specs=pl.BlockSpec(memory_space=HBM),
        scratch_shapes=[pltpu.VMEM((3, RB, T, C), F32), dma((3,))],
        compiler_params=params(),
        name="spread_near",
    )(z0, z1, up0, up1, down0, down1)
    return pl.pallas_call(
        spread_far_kernel,
        out_shape=whole,
        in_specs=[pl.BlockSpec(memory_space=VMEM)] * 2 + [pl.BlockSpec(memory_space=HBM)],
        out_specs=pl.BlockSpec(memory_space=HBM),
        scratch_shapes=[pltpu.VMEM((2, HB, T, C), F32), dma((2,))],
        input_output_aliases={2: 0},
        compiler_params=params(),
        name="spread_far",
    )(far0, far1, near)


def solution(mesh):
    placed = (
        P("row", None, None),
        P(),
        P(),
        P(),
        P(None, None, None, "ch"),
        P(),
        P(None, "ch"),
        P(None, "ch"),
        P(None, "ch", None),
    )
    return jax.shard_map(
        on_device, mesh=mesh, in_specs=placed, out_specs=P("row", None, None), check_vma=False
    )
```

```python
import functools

import jax
import jax.numpy as jnp
from jax import lax
from jax.experimental import pallas as pl
from jax.experimental.pallas import tpu as pltpu
from jax.sharding import PartitionSpec as P

F32, BF16 = jnp.float32, jnp.bfloat16
N, C, T = 512, 128, 128
RB = 16
G, R = 4, 32
D = C // G
HB = RB // 2
HBM, VMEM = pltpu.HBM, pltpu.VMEM
VMEM_LIMIT = 32 * 1024 * 1024
WHOLE_VMEM = 60 * 1024 * 1024
MOST_VMEM = 51 * 1024 * 1024

PK_PROJ, PK_OUT, PK_NORM, PK = 0, 128, 192, 208


def dot(a, b, ca=1, cb=0):
    return lax.dot_general(a, b, (((ca,), (cb,)), ((), ())), preferred_element_type=F32)


def column(row):
    return jnp.broadcast_to(row, (C, C)).T


def norm_cols(v, gain, bias):
    mean = jnp.mean(v, 0, keepdims=True)
    cent = v - mean
    var = jnp.mean(cent * cent, 0, keepdims=True)
    return cent * lax.rsqrt(var + 1e-05) * gain + bias


def sigmoid(v):
    return 0.5 * jnp.tanh(0.5 * v) + 0.5


def gated(gate, value, half_mask):
    return (jnp.tanh(0.5 * gate) + 1.0) * (value * half_mask)


def project0_kernel(
    pair, mask, in_gain, in_bias, w, w_out, out_gain, out_bias, out, own,
    rows, mask_v, mask_s, gb, w_v, wo_v, og_v, left_s, right_s, zn_s, sems,
):
    small = [
        (mask, mask_v),
        (mask, mask_s),
        (in_gain, gb.at[0]),
        (in_bias, gb.at[1]),
        (w, w_v),
        (w_out, wo_v),
        (out_gain, og_v.at[0]),
        (out_bias, og_v.at[1]),
    ]
    big = [(pair.at[:, pl.ds(T * h, T)], rows.at[h]) for h in range(G)]
    copies = [pltpu.make_async_copy(*ends, sems.at[k]) for k, ends in enumerate(small + big)]
    few = len(small)
    for copy in copies[few : few + 1] + copies[:few] + copies[few + 1 :]:
        copy.start()
    for copy in copies[:few]:
        copy.wait()
    gain, bias = column(gb[0, 0:1, :]), column(gb[1, 0:1, :])
    cols = mask_v[...].astype(F32) * 0.5
    row0 = lax.axis_index("row") * RB

    own[:PK_OUT] = w_v[1]
    own[PK_OUT:PK_NORM] = wo_v[...].reshape(2 * D, C)
    norms = jnp.concatenate([og_v[0], og_v[1]], 0)
    hi = norms.astype(BF16).astype(F32)
    mid = (norms - hi).astype(BF16).astype(F32)
    low = norms - hi - mid
    tile = jnp.concatenate([hi, mid, low, jnp.zeros_like(hi)], 0)
    own[PK_NORM:] = jnp.concatenate([tile, jnp.zeros((16, C - D), F32)], 1).astype(BF16)

    for h in range(G):
        copies[few + h].wait()
        for i in range(RB):
            zn_s[h, i] = norm_cols(rows[h, i].T, gain, bias).astype(BF16)
        for i in range(0, RB, 2):
            proj = dot(w_v[0], jnp.concatenate([zn_s[h, i], zn_s[h, i + 1]], 1))
            for k in (0, 1):
                half = cols[:, T * h : T * h + T] * mask_s[0, row0 + i + k].astype(F32)
                part = proj[:, T * k : T * k + T]
                left_s[h, pl.ds(i + k, D, stride=RB), :] = gated(part[0:D], part[D : 2 * D], half)
                right_s[h, pl.ds(i + k, D, stride=RB), :] = gated(part[2 * D : 3 * D], part[3 * D :], half)
        out[:, 0, :, T * h : T * h + T] = left_s[h].reshape(D, RB, T).astype(BF16)
        out[:, 1, :, T * h : T * h + T] = right_s[h].reshape(D, RB, T).astype(BF16)


def gate0_kernel(pair, mask, in_gain, in_bias, w_gate, state, gate, half, in_norm, block, mask_v, mask_s, sems):
    at = pl.multiple_of(lax.axis_index("ch") * T, T)
    copies = [
        pltpu.make_async_copy(pair.at[:, pl.ds(at, T), :], block, sems.at[0]),
        pltpu.make_async_copy(mask.at[:, pl.ds(at, T)], mask_v, sems.at[1]),
        pltpu.make_async_copy(mask, mask_s, sems.at[2]),
    ]
    for copy in copies:
        copy.start()
    gain, bias = column(in_gain[0:1, :]), column(in_bias[0:1, :])
    in_norm[0] = column(in_gain[1:2, :])
    in_norm[1] = column(in_bias[1:2, :])
    w_g = w_gate[0].astype(F32).T.astype(BF16)
    for copy in copies:
        copy.wait()
    row0 = lax.axis_index("row") * RB
    for i in range(RB):
        half[i : i + 1, :] = mask_v[...].astype(F32) * (0.5 * mask_s[0, row0 + i].astype(F32))
        z = block[i].T
        state[i] = z
        gate[i] = sigmoid(dot(w_g, norm_cols(z, gain, bias).astype(BF16)))


def weights_kernel(own, up, down, far, w_proj, w_out, norms, pk):
    g = lax.axis_index("ch")
    pk[g] = own[...]
    pk[lax.rem(g + 3, G)] = up[...]
    pk[lax.rem(g + 1, G)] = down[...]
    pk[lax.rem(g + 2, G)] = far[...]
    for k in range(G):
        w_proj[k] = pk[k, PK_PROJ : PK_PROJ + C]
    for k in range(G):
        parts = pk[k, PK_NORM:].astype(F32)
        parts = parts[0:4] + parts[4:8] + parts[8:12]
        for j in range(4):
            norms[j, D * k : D * k + D] = column(parts[j : j + 1])[:D]
    for layer in range(2):
        rows = jnp.concatenate(
            [pk[k, PK_OUT + D * layer : PK_OUT + D * (layer + 1)] for k in range(G)], 0
        )
        w_out[layer] = rows.astype(F32).T.astype(BF16)


def outgoing_kernel(a, out):
    left = a[:, 0].reshape(N, N)
    for h in range(G):
        right = a[8 * h : 8 * h + 8, 1].reshape(T, N)
        out[h] = dot(left, right, 1, 1).reshape(R, RB, T).astype(BF16)


def incoming_kernel(b, out):
    left = jnp.concatenate([b[R * h : R * h + R, 0].reshape(N, T) for h in range(G)], 1)
    for h in range(G):
        right = b[R * h : R * h + R, 1].reshape(N, T)
        out[h] = dot(left, right, 0, 0).reshape(R, RB, T).astype(BF16)


def middle_kernel(
    y, z0, gate, half_mask, in_norm, w_proj, w_out, norms, state, normed, out, ys, left_s, right_s, hid
):
    ys[...] = y[...].astype(F32).reshape(C * RB, T)
    for i in range(RB):
        hid[i] = norm_cols(ys[pl.ds(i, C, stride=RB), :], norms[0], norms[2]).astype(BF16)
    for i in range(RB):
        z = z0[i] + gate[i] * dot(w_out[0], hid[i])
        state[i] = z
        normed[i] = norm_cols(z, in_norm[0], in_norm[1]).astype(BF16)
    for g in range(G):
        for i in range(0, RB, 2):
            half = jnp.concatenate([half_mask[i : i + 1, :], half_mask[i + 1 : i + 2, :]], 1)
            proj = dot(w_proj[g], jnp.concatenate([normed[i], normed[i + 1]], 1))
            left = gated(proj[0:D], proj[D : 2 * D], half)
            right = gated(proj[2 * D : 3 * D], proj[3 * D :], half)
            for k in (0, 1):
                rows = pl.ds(i + k + g * D * RB, D, stride=RB)
                left_s[rows, :] = left[:, T * k : T * k + T]
                right_s[rows, :] = right[:, T * k : T * k + T]
    out[:, 0] = left_s[...].reshape(C, RB, T).astype(BF16)
    out[:, 1] = right_s[...].reshape(C, RB, T).astype(BF16)


def last_kernel(y, state, normed, w_gate, w_out, norms, out0, out1, ys):
    w_g = w_gate[1].astype(F32).T.astype(BF16)
    ys[...] = y[...].astype(F32).reshape(C * RB, T)
    for i in range(RB):
        hidden = norm_cols(ys[pl.ds(i, C, stride=RB), :], norms[1], norms[3]).astype(BF16)
        gate = sigmoid(dot(w_g, normed[i]))
        z = state[i] + gate * dot(w_out[1], hidden)
        out = (out0, out1)[i // HB]
        out[i % HB] = z.T.astype(BF16)


def spread_near_kernel(own0, own1, up0, up1, down0, down1, out, buf, sems):
    g = lax.axis_index("ch")
    copies = []
    for k, (shift, lo, hi) in enumerate([(0, own0, own1), (3, up0, up1), (1, down0, down1)]):
        buf[k, :HB] = lo[...].astype(F32)
        buf[k, HB:] = hi[...].astype(F32)
        at = pl.multiple_of(lax.rem(g + shift, G) * T, T)
        copies.append(pltpu.make_async_copy(buf.at[k], out.at[:, pl.ds(at, T), :], sems.at[k]))
        copies[-1].start()
    for copy in copies:
        copy.wait()


def spread_far_kernel(far0, far1, _, out, buf, sems):
    at = pl.multiple_of(lax.rem(lax.axis_index("ch") + 2, G) * T, T)
    copies = []
    for k, far in enumerate((far0, far1)):
        buf[k] = far[...].astype(F32)
        copies.append(
            pltpu.make_async_copy(buf.at[k], out.at[pl.ds(k * HB, HB), pl.ds(at, T), :], sems.at[k])
        )
        copies[-1].start()
    for copy in copies:
        copy.wait()


def params(limit=VMEM_LIMIT):
    return pltpu.CompilerParams(vmem_limit_bytes=limit)


def call(kernel, name, outs, scratch, ins, limit=VMEM_LIMIT):
    return pl.pallas_call(
        kernel,
        out_shape=outs,
        in_specs=[pl.BlockSpec(memory_space=space) for _, space in ins],
        out_specs=jax.tree.map(lambda _: pl.BlockSpec(memory_space=VMEM), outs),
        scratch_shapes=scratch,
        compiler_params=params(limit),
        name=name,
    )(*[value for value, _ in ins])


def on_device(pair, mask, in_gain, in_bias, w_proj, w_gate, out_gain, out_bias, w_out):
    arr = jax.ShapeDtypeStruct
    mask = mask[None]
    w_t = jnp.transpose(w_proj, (0, 2, 3, 1)).reshape(2, 4 * D, C)
    dma = pltpu.SemaphoreType.DMA

    a, own = call(
        project0_kernel,
        "project0",
        (arr((D, 2, RB, N), BF16), arr((PK, C), BF16)),
        [
            pltpu.VMEM((G, RB, T, C), F32),
            pltpu.VMEM((1, N), jnp.int32),
            pltpu.SMEM((1, N), jnp.int32),
            pltpu.VMEM((2, 2, C), F32),
            pltpu.VMEM((2, 4 * D, C), BF16),
            pltpu.VMEM((2, D, C), BF16),
            pltpu.VMEM((2, 2, D), F32),
            pltpu.VMEM((G, D * RB, T), F32),
            pltpu.VMEM((G, D * RB, T), F32),
            pltpu.VMEM((G, RB, C, T), BF16),
            dma((8 + G,)),
        ],
        [(v, HBM) for v in (pair, mask, in_gain, in_bias, w_t, w_out, out_gain, out_bias)],
        WHOLE_VMEM,
    )

    up = functools.partial(lax.ppermute, axis_name="ch", perm=[(k, (k + 1) % G) for k in range(G)])
    down = functools.partial(lax.ppermute, axis_name="ch", perm=[(k, (k - 1) % G) for k in range(G)])
    cross = functools.partial(lax.ppermute, axis_name="ch", perm=[(k, (k + 2) % G) for k in range(G)])

    a = lax.all_to_all(a, "row", 0, 0)
    w_proj1, w_out_t, norms = call(
        weights_kernel,
        "weights",
        (arr((G, C, C), BF16), arr((2, C, C), BF16), arr((4, C, T), F32)),
        [pltpu.VMEM((G, PK, C), BF16)],
        [(v, VMEM) for v in (own, up(own), down(own), cross(own))],
    )
    state, gate, half_mask, in_norm = call(
        gate0_kernel,
        "gate0",
        (arr((RB, C, T), F32), arr((RB, C, T), F32), arr((RB, T), F32), arr((2, C, T), F32)),
        [
            pltpu.VMEM((RB, T, C), F32),
            pltpu.VMEM((1, T), jnp.int32),
            pltpu.SMEM((1, N), jnp.int32),
            dma((3,)),
        ],
        [(pair, HBM), (mask, HBM), (in_gain, VMEM), (in_bias, VMEM), (w_gate, VMEM)],
        MOST_VMEM,
    )
    a, state, gate, half_mask, in_norm, w_proj1, w_out_t, norms = lax.optimization_barrier(
        (a, state, gate, half_mask, in_norm, w_proj1, w_out_t, norms)
    )
    x = call(outgoing_kernel, "outgoing", arr((G, R, RB, T), BF16), [], [(a, VMEM)])
    y = lax.all_to_all(x.reshape(G * R, RB, T), ("ch", "row"), 0, 0)
    state, normed, b = call(
        middle_kernel,
        "middle",
        (arr((RB, C, T), F32), arr((RB, C, T), BF16), arr((C, 2, RB, T), BF16)),
        [pltpu.VMEM((C * RB, T), F32)] * 3 + [pltpu.VMEM((RB, C, T), BF16)],
        [(v, VMEM) for v in (y, state, gate, half_mask, in_norm, w_proj1, w_out_t, norms)],
    )
    b = lax.all_to_all(b, ("ch", "row"), 0, 0)
    x = call(incoming_kernel, "incoming", arr((G, R, RB, T), BF16), [], [(b, VMEM)])
    y = lax.all_to_all(x.reshape(G * R, RB, T), ("ch", "row"), 0, 0)
    half = arr((HB, T, C), BF16)
    z0, z1 = call(
        last_kernel,
        "last",
        (half, half),
        [pltpu.VMEM((C * RB, T), F32)],
        [(v, VMEM) for v in (y, state, normed, w_gate, w_out_t, norms)],
    )
    up0, down1 = up(z0), down(z1)
    up1, down0 = up(z1), down(z0)
    far0, far1 = up(up0), down(down1)
    whole = arr((RB, N, C), F32)
    near = pl.pallas_call(
        spread_near_kernel,
        out_shape=whole,
        in_specs=[pl.BlockSpec(memory_space=VMEM)] * 6,
        out_specs=pl.BlockSpec(memory_space=HBM),
        scratch_shapes=[pltpu.VMEM((3, RB, T, C), F32), dma((3,))],
        compiler_params=params(),
        name="spread_near",
    )(z0, z1, up0, up1, down0, down1)
    return pl.pallas_call(
        spread_far_kernel,
        out_shape=whole,
        in_specs=[pl.BlockSpec(memory_space=VMEM)] * 2 + [pl.BlockSpec(memory_space=HBM)],
        out_specs=pl.BlockSpec(memory_space=HBM),
        scratch_shapes=[pltpu.VMEM((2, HB, T, C), F32), dma((2,))],
        input_output_aliases={2: 0},
        compiler_params=params(),
        name="spread_far",
    )(far0, far1, near)


def solution(mesh):
    placed = (
        P("row", None, None),
        P(),
        P(),
        P(),
        P(None, None, None, "ch"),
        P(),
        P(None, "ch"),
        P(None, "ch"),
        P(None, "ch", None),
    )
    return jax.shard_map(
        on_device, mesh=mesh, in_specs=placed, out_specs=P("row", None, None), check_vma=False
    )
```

```python
import functools

import jax
import jax.numpy as jnp
from jax import lax
from jax.experimental import pallas as pl
from jax.experimental.pallas import tpu as pltpu
from jax.sharding import PartitionSpec as P

F32, BF16 = jnp.float32, jnp.bfloat16
N, C, T = 512, 128, 128
RB = 16
G, R = 4, 32
D = C // G
HB = RB // 2
HBM, VMEM = pltpu.HBM, pltpu.VMEM
VMEM_LIMIT = 32 * 1024 * 1024
WHOLE_VMEM = 60 * 1024 * 1024
MOST_VMEM = 51 * 1024 * 1024

PK_PROJ, PK_OUT, PK_NORM, PK = 0, 128, 192, 208


def dot(a, b, ca=1, cb=0):
    return lax.dot_general(a, b, (((ca,), (cb,)), ((), ())), preferred_element_type=F32)


def column(row):
    return jnp.broadcast_to(row, (C, C)).T


def norm_cols(v, gain, bias):
    mean = jnp.mean(v, 0, keepdims=True)
    cent = v - mean
    var = jnp.mean(cent * cent, 0, keepdims=True)
    return cent * lax.rsqrt(var + 1e-05) * gain + bias


def sigmoid(v):
    return 0.5 * jnp.tanh(0.5 * v) + 0.5


def gated(gate, value, half_mask):
    return (jnp.tanh(0.5 * gate) + 1.0) * (value * half_mask)


def project0_kernel(
    pair, mask, in_gain, in_bias, w, out,
    rows, mask_v, mask_s, gb, w_v, left_s, right_s, zn_s, stage, sems,
):
    small = [(in_gain, gb.at[0]), (in_bias, gb.at[1]), (w.at[0], w_v), (mask, mask_v), (mask, mask_s)]
    big = [(pair.at[:, pl.ds(T * h, T)], rows.at[h]) for h in range(G)]
    copies = [pltpu.make_async_copy(*ends, sems.at[k]) for k, ends in enumerate(small + big)]
    few = len(small)
    for copy in copies[:2] + copies[few : few + 1] + copies[2:few] + copies[few + 1 :]:
        copy.start()
    for copy in copies[:2]:
        copy.wait()
    gain, bias = column(gb[0, 0:1, :]), column(gb[1, 0:1, :])
    row0 = lax.axis_index("row") * RB
    cols = None
    for h in range(G + 1):
        if h < G:
            copies[few + h].wait()
        if h == 1:
            for copy in copies[2:few]:
                copy.wait()
            cols = mask_v[...].astype(F32) * 0.5
        for i in range(0, RB, 2):
            if h < G:
                for k in (0, 1):
                    zn_s[h, i + k] = norm_cols(rows[h, i + k].T, gain, bias).astype(BF16)
            if h > 0:
                e = h - 1
                proj = dot(w_v[...], jnp.concatenate([zn_s[e, i], zn_s[e, i + 1]], 1))
                for k in (0, 1):
                    half = cols[:, T * e : T * e + T] * mask_s[0, row0 + i + k].astype(F32)
                    part = proj[:, T * k : T * k + T]
                    left_s[e, pl.ds(i + k, D, stride=RB), :] = gated(part[0:D], part[D : 2 * D], half)
                    right_s[e, pl.ds(i + k, D, stride=RB), :] = gated(part[2 * D : 3 * D], part[3 * D :], half)
        if h > 0:
            stage[e, :, 0] = left_s[e].reshape(D, RB, T).astype(BF16)
            stage[e, :, 1] = right_s[e].reshape(D, RB, T).astype(BF16)
            copies.append(
                pltpu.make_async_copy(stage.at[e], out.at[:, :, :, pl.ds(T * e, T)], sems.at[few + G + e])
            )
            copies[-1].start()
    for copy in copies[few + G :]:
        copy.wait()


def gate0_kernel(
    pair, mask, in_gain, in_bias, w_gate, w, w_out, out_gain, out_bias, state, gate, half, own, block, mask_v, mask_s, sems
):
    at = pl.multiple_of(lax.axis_index("ch") * T, T)
    copies = [
        pltpu.make_async_copy(pair.at[:, pl.ds(at, T), :], block, sems.at[0]),
        pltpu.make_async_copy(mask.at[:, pl.ds(at, T)], mask_v, sems.at[1]),
        pltpu.make_async_copy(mask, mask_s, sems.at[2]),
    ]
    for copy in copies:
        copy.start()
    own[:PK_OUT] = w[1]
    own[PK_OUT:PK_NORM] = w_out[...].reshape(2 * D, C)
    norms = jnp.concatenate([out_gain[...], out_bias[...]], 0)
    hi = norms.astype(BF16).astype(F32)
    mid = (norms - hi).astype(BF16).astype(F32)
    low = norms - hi - mid
    tile = jnp.concatenate([hi, mid, low, jnp.zeros_like(hi)], 0)
    own[PK_NORM:] = jnp.concatenate([tile, jnp.zeros((16, C - D), F32)], 1).astype(BF16)
    gain, bias = column(in_gain[0:1, :]), column(in_bias[0:1, :])
    w_g = w_gate[0].astype(F32).T.astype(BF16)
    for copy in copies:
        copy.wait()
    row0 = lax.axis_index("row") * RB
    for i in range(RB):
        half[i : i + 1, :] = mask_v[...].astype(F32) * (0.5 * mask_s[0, row0 + i].astype(F32))
        z = block[i].T
        state[i] = z
        gate[i] = sigmoid(dot(w_g, norm_cols(z, gain, bias).astype(BF16)))


def weights_kernel(own, up, down, far, in_gain, in_bias, w, norms, pk):
    g = lax.axis_index("ch")
    pk[g] = own[...]
    pk[lax.rem(g + 3, G)] = up[...]
    pk[lax.rem(g + 1, G)] = down[...]
    pk[lax.rem(g + 2, G)] = far[...]
    for k in range(G):
        w[k] = pk[k, PK_PROJ : PK_PROJ + C]
    for k in range(G):
        parts = pk[k, PK_NORM:].astype(F32)
        parts = parts[0:4] + parts[4:8] + parts[8:12]
        for j in range(4):
            norms[j, D * k : D * k + D] = column(parts[j : j + 1])[:D]
    for layer in range(2):
        rows = jnp.concatenate(
            [pk[k, PK_OUT + D * layer : PK_OUT + D * (layer + 1)] for k in range(G)], 0
        )
        w[G + layer] = rows.astype(F32).T.astype(BF16)
    norms[4] = column(in_gain[1:2, :])
    norms[5] = column(in_bias[1:2, :])


def outgoing_kernel(a, out):
    left = a[:, 0].reshape(N, N)
    for h in range(G):
        right = a[8 * h : 8 * h + 8, 1].reshape(T, N)
        out[h] = dot(left, right, 1, 1).reshape(R, RB, T).astype(BF16)


def incoming_kernel(b, out):
    left = jnp.concatenate([b[R * h : R * h + R, 0].reshape(N, T) for h in range(G)], 1)
    for h in range(G):
        right = b[R * h : R * h + R, 1].reshape(N, T)
        out[h] = dot(left, right, 0, 0).reshape(R, RB, T).astype(BF16)


def middle_kernel(
    y, z0, gate, half_mask, w, norms, state, normed, out, ys, left_s, right_s, hid
):
    ys[...] = y[...].astype(F32).reshape(C * RB, T)
    for i in range(RB):
        hid[i] = norm_cols(ys[pl.ds(i, C, stride=RB), :], norms[0], norms[2]).astype(BF16)
    for i in range(RB):
        z = z0[i] + gate[i] * dot(w[G], hid[i])
        state[i] = z
        normed[i] = norm_cols(z, norms[4], norms[5]).astype(BF16)
    for g in range(G):
        for i in range(0, RB, 2):
            half = jnp.concatenate([half_mask[i : i + 1, :], half_mask[i + 1 : i + 2, :]], 1)
            proj = dot(w[g], jnp.concatenate([normed[i], normed[i + 1]], 1))
            left = gated(proj[0:D], proj[D : 2 * D], half)
            right = gated(proj[2 * D : 3 * D], proj[3 * D :], half)
            for k in (0, 1):
                rows = pl.ds(i + k + g * D * RB, D, stride=RB)
                left_s[rows, :] = left[:, T * k : T * k + T]
                right_s[rows, :] = right[:, T * k : T * k + T]
    out[:, 0] = left_s[...].reshape(C, RB, T).astype(BF16)
    out[:, 1] = right_s[...].reshape(C, RB, T).astype(BF16)


def last_kernel(y, state, normed, w_gate, w, norms, out0, out1, ys):
    w_g = w_gate[1].astype(F32).T.astype(BF16)
    ys[...] = y[...].astype(F32).reshape(C * RB, T)
    for i in range(RB):
        hidden = norm_cols(ys[pl.ds(i, C, stride=RB), :], norms[1], norms[3]).astype(BF16)
        gate = sigmoid(dot(w_g, normed[i]))
        z = state[i] + gate * dot(w[G + 1], hidden)
        out = (out0, out1)[i // HB]
        out[i % HB] = z.T.astype(BF16)


def spread_near_kernel(own0, own1, up0, up1, down0, down1, out, buf, sems):
    g = lax.axis_index("ch")
    copies = []
    for k, (shift, lo, hi) in enumerate([(0, own0, own1), (3, up0, up1), (1, down0, down1)]):
        buf[k, :HB] = lo[...].astype(F32)
        buf[k, HB:] = hi[...].astype(F32)
        at = pl.multiple_of(lax.rem(g + shift, G) * T, T)
        copies.append(pltpu.make_async_copy(buf.at[k], out.at[:, pl.ds(at, T), :], sems.at[k]))
        copies[-1].start()
    for copy in copies:
        copy.wait()


def spread_far_kernel(far0, far1, _, out, buf, sems):
    at = pl.multiple_of(lax.rem(lax.axis_index("ch") + 2, G) * T, T)
    copies = []
    for k, far in enumerate((far0, far1)):
        buf[k] = far[...].astype(F32)
        copies.append(
            pltpu.make_async_copy(buf.at[k], out.at[pl.ds(k * HB, HB), pl.ds(at, T), :], sems.at[k])
        )
        copies[-1].start()
    for copy in copies:
        copy.wait()


def params(limit=VMEM_LIMIT):
    return pltpu.CompilerParams(vmem_limit_bytes=limit)


def call(kernel, name, outs, scratch, ins, limit=VMEM_LIMIT, out_space=None):
    return pl.pallas_call(
        kernel,
        out_shape=outs,
        in_specs=[pl.BlockSpec(memory_space=space) for _, space in ins],
        out_specs=jax.tree.map(lambda _: pl.BlockSpec(memory_space=out_space or VMEM), outs),
        scratch_shapes=scratch,
        compiler_params=params(limit),
        name=name,
    )(*[value for value, _ in ins])


def on_device(pair, mask, in_gain, in_bias, w_proj, w_gate, out_gain, out_bias, w_out):
    arr = jax.ShapeDtypeStruct
    mask = mask[None]
    w_t = jnp.transpose(w_proj, (0, 2, 3, 1)).reshape(2, 4 * D, C)
    dma = pltpu.SemaphoreType.DMA

    a = call(
        project0_kernel,
        "project0",
        arr((D, 2, RB, N), BF16),
        [
            pltpu.VMEM((G, RB, T, C), F32),
            pltpu.VMEM((1, N), jnp.int32),
            pltpu.SMEM((1, N), jnp.int32),
            pltpu.VMEM((2, 2, C), F32),
            pltpu.VMEM((4 * D, C), BF16),
            pltpu.VMEM((G, D * RB, T), F32),
            pltpu.VMEM((G, D * RB, T), F32),
            pltpu.VMEM((G, RB, C, T), BF16),
            pltpu.VMEM((G, D, 2, RB, T), BF16),
            dma((5 + 2 * G,)),
        ],
        [(v, HBM) for v in (pair, mask, in_gain, in_bias, w_t)],
        WHOLE_VMEM,
        HBM,
    )

    up = functools.partial(lax.ppermute, axis_name="ch", perm=[(k, (k + 1) % G) for k in range(G)])
    down = functools.partial(lax.ppermute, axis_name="ch", perm=[(k, (k - 1) % G) for k in range(G)])
    cross = functools.partial(lax.ppermute, axis_name="ch", perm=[(k, (k + 2) % G) for k in range(G)])

    sent = lax.all_to_all(a, "row", 0, 0)
    state, gate, half_mask, own = call(
        gate0_kernel,
        "gate0",
        (arr((RB, C, T), F32), arr((RB, C, T), F32), arr((RB, T), F32), arr((PK, C), BF16)),
        [
            pltpu.VMEM((RB, T, C), F32),
            pltpu.VMEM((1, T), jnp.int32),
            pltpu.SMEM((1, N), jnp.int32),
            dma((3,)),
        ],
        [(pair, HBM), (mask, HBM)]
        + [(v, VMEM) for v in (in_gain, in_bias, w_gate, w_t, w_out, out_gain, out_bias)],
        MOST_VMEM,
    )
    a, state, gate, half_mask, own = lax.optimization_barrier((sent, state, gate, half_mask, own))
    w, norms = call(
        weights_kernel,
        "weights",
        (arr((G + 2, C, C), BF16), arr((6, C, T), F32)),
        [pltpu.VMEM((G, PK, C), BF16)],
        [(v, VMEM) for v in (own, up(own), down(own), cross(own), in_gain, in_bias)],
    )
    x = call(outgoing_kernel, "outgoing", arr((G, R, RB, T), BF16), [], [(a, VMEM)])
    y = lax.all_to_all(x.reshape(G * R, RB, T), ("ch", "row"), 0, 0)
    state, normed, b = call(
        middle_kernel,
        "middle",
        (arr((RB, C, T), F32), arr((RB, C, T), BF16), arr((C, 2, RB, T), BF16)),
        [pltpu.VMEM((C * RB, T), F32)] * 3 + [pltpu.VMEM((RB, C, T), BF16)],
        [(v, VMEM) for v in (y, state, gate, half_mask, w, norms)],
    )
    b = lax.all_to_all(b, ("ch", "row"), 0, 0)
    x = call(incoming_kernel, "incoming", arr((G, R, RB, T), BF16), [], [(b, VMEM)])
    y = lax.all_to_all(x.reshape(G * R, RB, T), ("ch", "row"), 0, 0)
    half = arr((HB, T, C), BF16)
    z0, z1 = call(
        last_kernel,
        "last",
        (half, half),
        [pltpu.VMEM((C * RB, T), F32)],
        [(v, VMEM) for v in (y, state, normed, w_gate, w, norms)],
    )
    up0, down1 = up(z0), down(z1)
    up1, down0 = up(z1), down(z0)
    far0, far1 = up(up0), down(down1)
    whole = arr((RB, N, C), F32)
    near = pl.pallas_call(
        spread_near_kernel,
        out_shape=whole,
        in_specs=[pl.BlockSpec(memory_space=VMEM)] * 6,
        out_specs=pl.BlockSpec(memory_space=HBM),
        scratch_shapes=[pltpu.VMEM((3, RB, T, C), F32), dma((3,))],
        compiler_params=params(),
        name="spread_near",
    )(z0, z1, up0, up1, down0, down1)
    return pl.pallas_call(
        spread_far_kernel,
        out_shape=whole,
        in_specs=[pl.BlockSpec(memory_space=VMEM)] * 2 + [pl.BlockSpec(memory_space=HBM)],
        out_specs=pl.BlockSpec(memory_space=HBM),
        scratch_shapes=[pltpu.VMEM((2, HB, T, C), F32), dma((2,))],
        input_output_aliases={2: 0},
        compiler_params=params(),
        name="spread_far",
    )(far0, far1, near)


def solution(mesh):
    placed = (
        P("row", None, None),
        P(),
        P(),
        P(),
        P(None, None, None, "ch"),
        P(),
        P(None, "ch"),
        P(None, "ch"),
        P(None, "ch", None),
    )
    return jax.shard_map(
        on_device, mesh=mesh, in_specs=placed, out_specs=P("row", None, None), check_vma=False
    )
```

```python
import functools

import jax
import jax.numpy as jnp
from jax import lax
from jax.experimental import pallas as pl
from jax.experimental.pallas import tpu as pltpu
from jax.sharding import PartitionSpec as P

F32, BF16 = jnp.float32, jnp.bfloat16
N, C, T = 512, 128, 128
RB = 16
G, R = 4, 32
D = C // G
HB = RB // 2
HBM, VMEM = pltpu.HBM, pltpu.VMEM
VMEM_LIMIT = 32 * 1024 * 1024
WHOLE_VMEM = 60 * 1024 * 1024
MOST_VMEM = 51 * 1024 * 1024

PK_PROJ, PK_OUT, PK_NORM, PK = 0, 128, 192, 208


def dot(a, b, ca=1, cb=0):
    return lax.dot_general(a, b, (((ca,), (cb,)), ((), ())), preferred_element_type=F32)


def column(row):
    return jnp.broadcast_to(row, (C, C)).T


def norm_cols(v, gain, bias):
    mean = jnp.mean(v, 0, keepdims=True)
    cent = v - mean
    var = jnp.mean(cent * cent, 0, keepdims=True)
    return cent * lax.rsqrt(var + 1e-05) * gain + bias


def sigmoid(v):
    return 0.5 * jnp.tanh(0.5 * v) + 0.5


def gated(gate, value, half_mask):
    return (jnp.tanh(0.5 * gate) + 1.0) * (value * half_mask)


def project0_kernel(
    pair, mask, in_gain, in_bias, w, out,
    rows, mask_v, mask_s, gb, w_v, left_s, right_s, zn_s, stage, sems,
):
    small = [(in_gain, gb.at[0]), (in_bias, gb.at[1]), (w.at[0], w_v), (mask, mask_v), (mask, mask_s)]
    big = [(pair.at[:, pl.ds(T * h, T)], rows.at[h]) for h in range(G)]
    copies = [pltpu.make_async_copy(*ends, sems.at[k]) for k, ends in enumerate(small + big)]
    few = len(small)
    for copy in copies[:2] + copies[few : few + 1] + copies[2:few] + copies[few + 1 :]:
        copy.start()
    for copy in copies[:2]:
        copy.wait()
    gain, bias = column(gb[0, 0:1, :]), column(gb[1, 0:1, :])
    row0 = lax.axis_index("row") * RB
    cols = None
    for h in range(G + 1):
        if h < G:
            copies[few + h].wait()
        if h == 1:
            for copy in copies[2:few]:
                copy.wait()
            cols = mask_v[...].astype(F32) * 0.5
        for i in range(0, RB, 2):
            if h < G:
                for k in (0, 1):
                    zn_s[h, i + k] = norm_cols(rows[h, i + k].T, gain, bias).astype(BF16)
            if h > 0:
                e = h - 1
                proj = dot(w_v[...], jnp.concatenate([zn_s[e, i], zn_s[e, i + 1]], 1))
                for k in (0, 1):
                    half = cols[:, T * e : T * e + T] * mask_s[0, row0 + i + k].astype(F32)
                    part = proj[:, T * k : T * k + T]
                    left_s[e, pl.ds(i + k, D, stride=RB), :] = gated(part[0:D], part[D : 2 * D], half)
                    right_s[e, pl.ds(i + k, D, stride=RB), :] = gated(part[2 * D : 3 * D], part[3 * D :], half)
        if h > 0:
            stage[e, :, 0] = left_s[e].reshape(D, RB, T).astype(BF16)
            stage[e, :, 1] = right_s[e].reshape(D, RB, T).astype(BF16)
            copies.append(
                pltpu.make_async_copy(stage.at[e], out.at[:, :, :, pl.ds(T * e, T)], sems.at[few + G + e])
            )
            copies[-1].start()
    for copy in copies[few + G :]:
        copy.wait()


def gate0_kernel(
    pair, mask, in_gain, in_bias, w_gate, w, w_out, out_gain, out_bias, state, gate, half, own, block, mask_v, mask_s, sems
):
    at = pl.multiple_of(lax.axis_index("ch") * T, T)
    copies = [
        pltpu.make_async_copy(pair.at[:, pl.ds(at, T), :], block, sems.at[0]),
        pltpu.make_async_copy(mask.at[:, pl.ds(at, T)], mask_v, sems.at[1]),
        pltpu.make_async_copy(mask, mask_s, sems.at[2]),
    ]
    for copy in copies:
        copy.start()
    own[:PK_OUT] = w[1]
    own[PK_OUT:PK_NORM] = w_out[...].reshape(2 * D, C)
    norms = jnp.concatenate([out_gain[...], out_bias[...]], 0)
    hi = norms.astype(BF16).astype(F32)
    mid = (norms - hi).astype(BF16).astype(F32)
    low = norms - hi - mid
    tile = jnp.concatenate([hi, mid, low, jnp.zeros_like(hi)], 0)
    own[PK_NORM:] = jnp.concatenate([tile, jnp.zeros((16, C - D), F32)], 1).astype(BF16)
    gain, bias = column(in_gain[0:1, :]), column(in_bias[0:1, :])
    w_g = w_gate[0].astype(F32).T.astype(BF16)
    for copy in copies:
        copy.wait()
    row0 = lax.axis_index("row") * RB
    for i in range(RB):
        half[i : i + 1, :] = mask_v[...].astype(F32) * (0.5 * mask_s[0, row0 + i].astype(F32))
        z = block[i].T
        state[i] = z
        gate[i] = sigmoid(dot(w_g, norm_cols(z, gain, bias).astype(BF16)))


def weights_kernel(own, up, down, far, in_gain, in_bias, w, norms, pk):
    g = lax.axis_index("ch")
    pk[g] = own[...]
    pk[lax.rem(g + 3, G)] = up[...]
    pk[lax.rem(g + 1, G)] = down[...]
    pk[lax.rem(g + 2, G)] = far[...]
    for k in range(G):
        w[k] = pk[k, PK_PROJ : PK_PROJ + C]
    for k in range(G):
        parts = pk[k, PK_NORM:].astype(F32)
        parts = parts[0:4] + parts[4:8] + parts[8:12]
        for j in range(4):
            norms[j, D * k : D * k + D] = column(parts[j : j + 1])[:D]
    for layer in range(2):
        rows = jnp.concatenate(
            [pk[k, PK_OUT + D * layer : PK_OUT + D * (layer + 1)] for k in range(G)], 0
        )
        w[G + layer] = rows.astype(F32).T.astype(BF16)
    norms[4] = column(in_gain[1:2, :])
    norms[5] = column(in_bias[1:2, :])


def outgoing_kernel(a, _w, _gate, out):
    left = a[:, 0].reshape(N, N)
    for h in range(G):
        right = a[8 * h : 8 * h + 8, 1].reshape(T, N)
        out[h] = dot(left, right, 1, 1).reshape(R, RB, T).astype(BF16)


def incoming_kernel(b, out):
    left = jnp.concatenate([b[R * h : R * h + R, 0].reshape(N, T) for h in range(G)], 1)
    for h in range(G):
        right = b[R * h : R * h + R, 1].reshape(N, T)
        out[h] = dot(left, right, 0, 0).reshape(R, RB, T).astype(BF16)


def middle_kernel(
    y, z0, gate, half_mask, w, norms, state, normed, out, ys, left_s, right_s, hid
):
    ys[...] = y[...].astype(F32).reshape(C * RB, T)
    for i in range(RB):
        hid[i] = norm_cols(ys[pl.ds(i, C, stride=RB), :], norms[0], norms[2]).astype(BF16)
    for i in range(RB):
        z = z0[i] + gate[i] * dot(w[G], hid[i])
        state[i] = z
        normed[i] = norm_cols(z, norms[4], norms[5]).astype(BF16)
    for g in range(G):
        for i in range(0, RB, 2):
            half = jnp.concatenate([half_mask[i : i + 1, :], half_mask[i + 1 : i + 2, :]], 1)
            proj = dot(w[g], jnp.concatenate([normed[i], normed[i + 1]], 1))
            left = gated(proj[0:D], proj[D : 2 * D], half)
            right = gated(proj[2 * D : 3 * D], proj[3 * D :], half)
            for k in (0, 1):
                rows = pl.ds(i + k + g * D * RB, D, stride=RB)
                left_s[rows, :] = left[:, T * k : T * k + T]
                right_s[rows, :] = right[:, T * k : T * k + T]
    out[:, 0] = left_s[...].reshape(C, RB, T).astype(BF16)
    out[:, 1] = right_s[...].reshape(C, RB, T).astype(BF16)


def last_kernel(y, state, normed, w_gate, w, norms, out0, out1, ys):
    w_g = w_gate[1].astype(F32).T.astype(BF16)
    ys[...] = y[...].astype(F32).reshape(C * RB, T)
    for i in range(RB):
        hidden = norm_cols(ys[pl.ds(i, C, stride=RB), :], norms[1], norms[3]).astype(BF16)
        gate = sigmoid(dot(w_g, normed[i]))
        z = state[i] + gate * dot(w[G + 1], hidden)
        out = (out0, out1)[i // HB]
        out[i % HB] = z.T.astype(BF16)


def spread_near_kernel(own0, own1, up0, up1, down0, down1, out, buf, sems):
    g = lax.axis_index("ch")
    copies = []
    for k, (shift, lo, hi) in enumerate([(0, own0, own1), (3, up0, up1), (1, down0, down1)]):
        buf[k, :HB] = lo[...].astype(F32)
        buf[k, HB:] = hi[...].astype(F32)
        at = pl.multiple_of(lax.rem(g + shift, G) * T, T)
        copies.append(pltpu.make_async_copy(buf.at[k], out.at[:, pl.ds(at, T), :], sems.at[k]))
        copies[-1].start()
    for copy in copies:
        copy.wait()


def spread_far_kernel(far0, far1, _, out, buf, sems):
    at = pl.multiple_of(lax.rem(lax.axis_index("ch") + 2, G) * T, T)
    copies = []
    for k, far in enumerate((far0, far1)):
        buf[k] = far[...].astype(F32)
        copies.append(
            pltpu.make_async_copy(buf.at[k], out.at[pl.ds(k * HB, HB), pl.ds(at, T), :], sems.at[k])
        )
        copies[-1].start()
    for copy in copies:
        copy.wait()


def params(limit=VMEM_LIMIT):
    return pltpu.CompilerParams(vmem_limit_bytes=limit)


def call(kernel, name, outs, scratch, ins, limit=VMEM_LIMIT, out_space=None):
    return pl.pallas_call(
        kernel,
        out_shape=outs,
        in_specs=[pl.BlockSpec(memory_space=space) for _, space in ins],
        out_specs=jax.tree.map(lambda _: pl.BlockSpec(memory_space=out_space or VMEM), outs),
        scratch_shapes=scratch,
        compiler_params=params(limit),
        name=name,
    )(*[value for value, _ in ins])


def on_device(pair, mask, in_gain, in_bias, w_proj, w_gate, out_gain, out_bias, w_out):
    arr = jax.ShapeDtypeStruct
    mask = mask[None]
    w_t = jnp.transpose(w_proj, (0, 2, 3, 1)).reshape(2, 4 * D, C)
    dma = pltpu.SemaphoreType.DMA

    a = call(
        project0_kernel,
        "project0",
        arr((D, 2, RB, N), BF16),
        [
            pltpu.VMEM((G, RB, T, C), F32),
            pltpu.VMEM((1, N), jnp.int32),
            pltpu.SMEM((1, N), jnp.int32),
            pltpu.VMEM((2, 2, C), F32),
            pltpu.VMEM((4 * D, C), BF16),
            pltpu.VMEM((G, D * RB, T), F32),
            pltpu.VMEM((G, D * RB, T), F32),
            pltpu.VMEM((G, RB, C, T), BF16),
            pltpu.VMEM((G, D, 2, RB, T), BF16),
            dma((5 + 2 * G,)),
        ],
        [(v, HBM) for v in (pair, mask, in_gain, in_bias, w_t)],
        WHOLE_VMEM,
        HBM,
    )

    up = functools.partial(lax.ppermute, axis_name="ch", perm=[(k, (k + 1) % G) for k in range(G)])
    down = functools.partial(lax.ppermute, axis_name="ch", perm=[(k, (k - 1) % G) for k in range(G)])
    cross = functools.partial(lax.ppermute, axis_name="ch", perm=[(k, (k + 2) % G) for k in range(G)])

    sent = lax.all_to_all(a, "row", 0, 0)
    state, gate, half_mask, own = call(
        gate0_kernel,
        "gate0",
        (arr((RB, C, T), F32), arr((RB, C, T), F32), arr((RB, T), F32), arr((PK, C), BF16)),
        [
            pltpu.VMEM((RB, T, C), F32),
            pltpu.VMEM((1, T), jnp.int32),
            pltpu.SMEM((1, N), jnp.int32),
            dma((3,)),
        ],
        [(pair, HBM), (mask, HBM)]
        + [(v, VMEM) for v in (in_gain, in_bias, w_gate, w_t, w_out, out_gain, out_bias)],
        MOST_VMEM,
    )
    w, norms = call(
        weights_kernel,
        "weights",
        (arr((G + 2, C, C), BF16), arr((6, C, T), F32)),
        [pltpu.VMEM((G, PK, C), BF16)],
        [(v, VMEM) for v in (own, up(own), down(own), cross(own), in_gain, in_bias)],
    )
    x = call(
        outgoing_kernel,
        "outgoing",
        arr((G, R, RB, T), BF16),
        [],
        [(sent, VMEM)] + [(v, pl.ANY) for v in (w, gate)],
    )
    y = lax.all_to_all(x.reshape(G * R, RB, T), ("ch", "row"), 0, 0)
    state, normed, b = call(
        middle_kernel,
        "middle",
        (arr((RB, C, T), F32), arr((RB, C, T), BF16), arr((C, 2, RB, T), BF16)),
        [pltpu.VMEM((C * RB, T), F32)] * 3 + [pltpu.VMEM((RB, C, T), BF16)],
        [(v, VMEM) for v in (y, state, gate, half_mask, w, norms)],
    )
    b = lax.all_to_all(b, ("ch", "row"), 0, 0)
    x = call(incoming_kernel, "incoming", arr((G, R, RB, T), BF16), [], [(b, VMEM)])
    y = lax.all_to_all(x.reshape(G * R, RB, T), ("ch", "row"), 0, 0)
    half = arr((HB, T, C), BF16)
    z0, z1 = call(
        last_kernel,
        "last",
        (half, half),
        [pltpu.VMEM((C * RB, T), F32)],
        [(v, VMEM) for v in (y, state, normed, w_gate, w, norms)],
    )
    up0, down1 = up(z0), down(z1)
    up1, down0 = up(z1), down(z0)
    far0, far1 = up(up0), down(down1)
    whole = arr((RB, N, C), F32)
    near = pl.pallas_call(
        spread_near_kernel,
        out_shape=whole,
        in_specs=[pl.BlockSpec(memory_space=VMEM)] * 6,
        out_specs=pl.BlockSpec(memory_space=HBM),
        scratch_shapes=[pltpu.VMEM((3, RB, T, C), F32), dma((3,))],
        compiler_params=params(),
        name="spread_near",
    )(z0, z1, up0, up1, down0, down1)
    return pl.pallas_call(
        spread_far_kernel,
        out_shape=whole,
        in_specs=[pl.BlockSpec(memory_space=VMEM)] * 2 + [pl.BlockSpec(memory_space=HBM)],
        out_specs=pl.BlockSpec(memory_space=HBM),
        scratch_shapes=[pltpu.VMEM((2, HB, T, C), F32), dma((2,))],
        input_output_aliases={2: 0},
        compiler_params=params(),
        name="spread_far",
    )(far0, far1, near)


def solution(mesh):
    placed = (
        P("row", None, None),
        P(),
        P(),
        P(),
        P(None, None, None, "ch"),
        P(),
        P(None, "ch"),
        P(None, "ch"),
        P(None, "ch", None),
    )
    return jax.shard_map(
        on_device, mesh=mesh, in_specs=placed, out_specs=P("row", None, None), check_vma=False
    )
```

```python
import functools

import jax
import jax.numpy as jnp
from jax import lax
from jax.experimental import pallas as pl
from jax.experimental.pallas import tpu as pltpu
from jax.sharding import PartitionSpec as P

F32, BF16 = jnp.float32, jnp.bfloat16
N, C, T = 512, 128, 128
RB = 16
G, R = 4, 32
D = C // G
HB = RB // 2
HBM, VMEM = pltpu.HBM, pltpu.VMEM
VMEM_LIMIT = 32 * 1024 * 1024
WHOLE_VMEM = 60 * 1024 * 1024
MOST_VMEM = 51 * 1024 * 1024

PK_PROJ, PK_OUT, PK_NORM, PK = 0, 128, 192, 208


def dot(a, b, ca=1, cb=0):
    return lax.dot_general(a, b, (((ca,), (cb,)), ((), ())), preferred_element_type=F32)


def column(row):
    return jnp.broadcast_to(row, (C, C)).T


def norm_cols(v, gain, bias):
    mean = jnp.mean(v, 0, keepdims=True)
    cent = v - mean
    var = jnp.mean(cent * cent, 0, keepdims=True)
    return cent * lax.rsqrt(var + 1e-05) * gain + bias


def sigmoid(v):
    return 0.5 * jnp.tanh(0.5 * v) + 0.5


def gated(gate, value, half_mask):
    return (jnp.tanh(0.5 * gate) + 1.0) * (value * half_mask)


def project0_kernel(
    pair, mask, in_gain, in_bias, w, out,
    rows, mask_v, mask_s, gb, w_v, left_s, right_s, zn_s, stage, sems,
):
    small = [(in_gain, gb.at[0]), (in_bias, gb.at[1]), (w.at[0], w_v), (mask, mask_v), (mask, mask_s)]
    big = [(pair.at[:, pl.ds(T * h, T)], rows.at[h]) for h in range(G)]
    copies = [pltpu.make_async_copy(*ends, sems.at[k]) for k, ends in enumerate(small + big)]
    few = len(small)
    for copy in copies[:2] + copies[few : few + 1] + copies[2:few] + copies[few + 1 :]:
        copy.start()
    for copy in copies[:2]:
        copy.wait()
    gain, bias = column(gb[0, 0:1, :]), column(gb[1, 0:1, :])
    row0 = lax.axis_index("row") * RB
    cols = None
    for h in range(G + 1):
        if h < G:
            copies[few + h].wait()
        if h == 1:
            for copy in copies[2:few]:
                copy.wait()
            cols = mask_v[...].astype(F32) * 0.5
        for i in range(0, RB, 2):
            if h < G:
                for k in (0, 1):
                    zn_s[h, i + k] = norm_cols(rows[h, i + k].T, gain, bias).astype(BF16)
            if h > 0:
                e = h - 1
                proj = dot(w_v[...], jnp.concatenate([zn_s[e, i], zn_s[e, i + 1]], 1))
                for k in (0, 1):
                    half = cols[:, T * e : T * e + T] * mask_s[0, row0 + i + k].astype(F32)
                    part = proj[:, T * k : T * k + T]
                    left_s[e, pl.ds(i + k, D, stride=RB), :] = gated(part[0:D], part[D : 2 * D], half)
                    right_s[e, pl.ds(i + k, D, stride=RB), :] = gated(part[2 * D : 3 * D], part[3 * D :], half)
        if h > 0:
            stage[e, :, 0] = left_s[e].reshape(D, RB, T).astype(BF16)
            stage[e, :, 1] = right_s[e].reshape(D, RB, T).astype(BF16)
            copies.append(
                pltpu.make_async_copy(stage.at[e], out.at[:, :, :, pl.ds(T * e, T)], sems.at[few + G + e])
            )
            copies[-1].start()
    for copy in copies[few + G :]:
        copy.wait()


def gate0_kernel(
    pair, mask, in_gain, in_bias, w_gate, w, w_out, out_gain, out_bias, state, gate, half, own, block, mask_v, mask_s, sems
):
    at = pl.multiple_of(lax.axis_index("ch") * T, T)
    copies = [
        pltpu.make_async_copy(pair.at[:, pl.ds(at, T), :], block, sems.at[0]),
        pltpu.make_async_copy(mask.at[:, pl.ds(at, T)], mask_v, sems.at[1]),
        pltpu.make_async_copy(mask, mask_s, sems.at[2]),
    ]
    for copy in copies:
        copy.start()
    own[:PK_OUT] = w[1]
    own[PK_OUT:PK_NORM] = w_out[...].reshape(2 * D, C)
    norms = jnp.concatenate([out_gain[...], out_bias[...]], 0)
    hi = norms.astype(BF16).astype(F32)
    mid = (norms - hi).astype(BF16).astype(F32)
    low = norms - hi - mid
    tile = jnp.concatenate([hi, mid, low, jnp.zeros_like(hi)], 0)
    own[PK_NORM:] = jnp.concatenate([tile, jnp.zeros((16, C - D), F32)], 1).astype(BF16)
    gain, bias = column(in_gain[0:1, :]), column(in_bias[0:1, :])
    w_g = w_gate[0].astype(F32).T.astype(BF16)
    for copy in copies:
        copy.wait()
    row0 = lax.axis_index("row") * RB
    for i in range(RB):
        half[i : i + 1, :] = mask_v[...].astype(F32) * (0.5 * mask_s[0, row0 + i].astype(F32))
        z = block[i].T
        state[i] = z
        gate[i] = sigmoid(dot(w_g, norm_cols(z, gain, bias).astype(BF16)))


def weights_kernel(own, up, down, far, in_gain, in_bias, w, norms, pk):
    g = lax.axis_index("ch")
    pk[g] = own[...]
    pk[lax.rem(g + 3, G)] = up[...]
    pk[lax.rem(g + 1, G)] = down[...]
    pk[lax.rem(g + 2, G)] = far[...]
    for k in range(G):
        w[k] = pk[k, PK_PROJ : PK_PROJ + C]
    for k in range(G):
        parts = pk[k, PK_NORM:].astype(F32)
        parts = parts[0:4] + parts[4:8] + parts[8:12]
        for j in range(4):
            norms[j, D * k : D * k + D] = column(parts[j : j + 1])[:D]
    for layer in range(2):
        rows = jnp.concatenate(
            [pk[k, PK_OUT + D * layer : PK_OUT + D * (layer + 1)] for k in range(G)], 0
        )
        w[G + layer] = rows.astype(F32).T.astype(BF16)
    norms[4] = column(in_gain[1:2, :])
    norms[5] = column(in_bias[1:2, :])


def outgoing_kernel(a, _w, _gate, out):
    left = a[:, 0].reshape(N, N)
    for h in range(0, G, 4):
        right = a[8 * h : 8 * (h + 4), 1].reshape(T * 4, N)
        x = dot(left, right, 1, 1)
        for k in range(4):
            out[h + k] = x[:, T * k : T * k + T].reshape(R, RB, T).astype(BF16)


def incoming_kernel(b, out):
    def columns(part, h, n):
        return jnp.concatenate([b[R * k : R * k + R, part].reshape(N, T) for k in range(h, h + n)], 1)

    left = columns(0, 0, G)
    for h in range(0, G, 4):
        x = dot(left, columns(1, h, 4), 0, 0)
        for k in range(4):
            out[h + k] = x[:, T * k : T * k + T].reshape(R, RB, T).astype(BF16)


def middle_kernel(
    y, z0, gate, half_mask, w, norms, state, normed, out, ys, left_s, right_s, hid
):
    ys[...] = y[...].astype(F32).reshape(C * RB, T)
    for i in range(RB):
        hid[i] = norm_cols(ys[pl.ds(i, C, stride=RB), :], norms[0], norms[2]).astype(BF16)
    for i in range(RB):
        z = z0[i] + gate[i] * dot(w[G], hid[i])
        state[i] = z
        normed[i] = norm_cols(z, norms[4], norms[5]).astype(BF16)
    for g in range(G):
        for i in range(0, RB, 2):
            half = jnp.concatenate([half_mask[i : i + 1, :], half_mask[i + 1 : i + 2, :]], 1)
            proj = dot(w[g], jnp.concatenate([normed[i], normed[i + 1]], 1))
            left = gated(proj[0:D], proj[D : 2 * D], half)
            right = gated(proj[2 * D : 3 * D], proj[3 * D :], half)
            for k in (0, 1):
                rows = pl.ds(i + k + g * D * RB, D, stride=RB)
                left_s[rows, :] = left[:, T * k : T * k + T]
                right_s[rows, :] = right[:, T * k : T * k + T]
    out[:, 0] = left_s[...].reshape(C, RB, T).astype(BF16)
    out[:, 1] = right_s[...].reshape(C, RB, T).astype(BF16)


def last_kernel(y, state, normed, w_gate, w, norms, out0, out1, ys):
    w_g = w_gate[1].astype(F32).T.astype(BF16)
    ys[...] = y[...].astype(F32).reshape(C * RB, T)
    for i in range(RB):
        hidden = norm_cols(ys[pl.ds(i, C, stride=RB), :], norms[1], norms[3]).astype(BF16)
        gate = sigmoid(dot(w_g, normed[i]))
        z = state[i] + gate * dot(w[G + 1], hidden)
        out = (out0, out1)[i // HB]
        out[i % HB] = z.T.astype(BF16)


def spread_near_kernel(own0, own1, up0, up1, down0, down1, out, buf, sems):
    g = lax.axis_index("ch")
    copies = []
    for k, (shift, lo, hi) in enumerate([(0, own0, own1), (3, up0, up1), (1, down0, down1)]):
        buf[k, :HB] = lo[...].astype(F32)
        buf[k, HB:] = hi[...].astype(F32)
        at = pl.multiple_of(lax.rem(g + shift, G) * T, T)
        copies.append(pltpu.make_async_copy(buf.at[k], out.at[:, pl.ds(at, T), :], sems.at[k]))
        copies[-1].start()
    for copy in copies:
        copy.wait()


def spread_far_kernel(far0, far1, _, out, buf, sems):
    at = pl.multiple_of(lax.rem(lax.axis_index("ch") + 2, G) * T, T)
    copies = []
    for k, far in enumerate((far0, far1)):
        buf[k] = far[...].astype(F32)
        copies.append(
            pltpu.make_async_copy(buf.at[k], out.at[pl.ds(k * HB, HB), pl.ds(at, T), :], sems.at[k])
        )
        copies[-1].start()
    for copy in copies:
        copy.wait()


def params(limit=VMEM_LIMIT):
    return pltpu.CompilerParams(vmem_limit_bytes=limit)


def call(kernel, name, outs, scratch, ins, limit=VMEM_LIMIT, out_space=None):
    return pl.pallas_call(
        kernel,
        out_shape=outs,
        in_specs=[pl.BlockSpec(memory_space=space) for _, space in ins],
        out_specs=jax.tree.map(lambda _: pl.BlockSpec(memory_space=out_space or VMEM), outs),
        scratch_shapes=scratch,
        compiler_params=params(limit),
        name=name,
    )(*[value for value, _ in ins])


def on_device(pair, mask, in_gain, in_bias, w_proj, w_gate, out_gain, out_bias, w_out):
    arr = jax.ShapeDtypeStruct
    mask = mask[None]
    w_t = jnp.transpose(w_proj, (0, 2, 3, 1)).reshape(2, 4 * D, C)
    dma = pltpu.SemaphoreType.DMA

    a = call(
        project0_kernel,
        "project0",
        arr((D, 2, RB, N), BF16),
        [
            pltpu.VMEM((G, RB, T, C), F32),
            pltpu.VMEM((1, N), jnp.int32),
            pltpu.SMEM((1, N), jnp.int32),
            pltpu.VMEM((2, 2, C), F32),
            pltpu.VMEM((4 * D, C), BF16),
            pltpu.VMEM((G, D * RB, T), F32),
            pltpu.VMEM((G, D * RB, T), F32),
            pltpu.VMEM((G, RB, C, T), BF16),
            pltpu.VMEM((G, D, 2, RB, T), BF16),
            dma((5 + 2 * G,)),
        ],
        [(v, HBM) for v in (pair, mask, in_gain, in_bias, w_t)],
        WHOLE_VMEM,
        HBM,
    )

    up = functools.partial(lax.ppermute, axis_name="ch", perm=[(k, (k + 1) % G) for k in range(G)])
    down = functools.partial(lax.ppermute, axis_name="ch", perm=[(k, (k - 1) % G) for k in range(G)])
    cross = functools.partial(lax.ppermute, axis_name="ch", perm=[(k, (k + 2) % G) for k in range(G)])

    sent = lax.all_to_all(a, "row", 0, 0)
    state, gate, half_mask, own = call(
        gate0_kernel,
        "gate0",
        (arr((RB, C, T), F32), arr((RB, C, T), F32), arr((RB, T), F32), arr((PK, C), BF16)),
        [
            pltpu.VMEM((RB, T, C), F32),
            pltpu.VMEM((1, T), jnp.int32),
            pltpu.SMEM((1, N), jnp.int32),
            dma((3,)),
        ],
        [(pair, HBM), (mask, HBM)]
        + [(v, VMEM) for v in (in_gain, in_bias, w_gate, w_t, w_out, out_gain, out_bias)],
        MOST_VMEM,
    )
    w, norms = call(
        weights_kernel,
        "weights",
        (arr((G + 2, C, C), BF16), arr((6, C, T), F32)),
        [pltpu.VMEM((G, PK, C), BF16)],
        [(v, VMEM) for v in (own, up(own), down(own), cross(own), in_gain, in_bias)],
    )
    x = call(
        outgoing_kernel,
        "outgoing",
        arr((G, R, RB, T), BF16),
        [],
        [(sent, VMEM)] + [(v, pl.ANY) for v in (w, gate)],
    )
    y = lax.all_to_all(x.reshape(G * R, RB, T), ("ch", "row"), 0, 0)
    state, normed, b = call(
        middle_kernel,
        "middle",
        (arr((RB, C, T), F32), arr((RB, C, T), BF16), arr((C, 2, RB, T), BF16)),
        [pltpu.VMEM((C * RB, T), F32)] * 3 + [pltpu.VMEM((RB, C, T), BF16)],
        [(v, VMEM) for v in (y, state, gate, half_mask, w, norms)],
    )
    b = lax.all_to_all(b, ("ch", "row"), 0, 0)
    x = call(incoming_kernel, "incoming", arr((G, R, RB, T), BF16), [], [(b, VMEM)])
    y = lax.all_to_all(x.reshape(G * R, RB, T), ("ch", "row"), 0, 0)
    half = arr((HB, T, C), BF16)
    z0, z1 = call(
        last_kernel,
        "last",
        (half, half),
        [pltpu.VMEM((C * RB, T), F32)],
        [(v, VMEM) for v in (y, state, normed, w_gate, w, norms)],
    )
    up0, down1 = up(z0), down(z1)
    up1, down0 = up(z1), down(z0)
    far0, far1 = up(up0), down(down1)
    whole = arr((RB, N, C), F32)
    near = pl.pallas_call(
        spread_near_kernel,
        out_shape=whole,
        in_specs=[pl.BlockSpec(memory_space=VMEM)] * 6,
        out_specs=pl.BlockSpec(memory_space=HBM),
        scratch_shapes=[pltpu.VMEM((3, RB, T, C), F32), dma((3,))],
        compiler_params=params(),
        name="spread_near",
    )(z0, z1, up0, up1, down0, down1)
    return pl.pallas_call(
        spread_far_kernel,
        out_shape=whole,
        in_specs=[pl.BlockSpec(memory_space=VMEM)] * 2 + [pl.BlockSpec(memory_space=HBM)],
        out_specs=pl.BlockSpec(memory_space=HBM),
        scratch_shapes=[pltpu.VMEM((2, HB, T, C), F32), dma((2,))],
        input_output_aliases={2: 0},
        compiler_params=params(),
        name="spread_far",
    )(far0, far1, near)


def solution(mesh):
    placed = (
        P("row", None, None),
        P(),
        P(),
        P(),
        P(None, None, None, "ch"),
        P(),
        P(None, "ch"),
        P(None, "ch"),
        P(None, "ch", None),
    )
    return jax.shard_map(
        on_device, mesh=mesh, in_specs=placed, out_specs=P("row", None, None), check_vma=False
    )
```

```python
import functools

import jax
import jax.numpy as jnp
from jax import lax
from jax.experimental import pallas as pl
from jax.experimental.pallas import tpu as pltpu
from jax.sharding import PartitionSpec as P

F32, BF16 = jnp.float32, jnp.bfloat16
N, C, T = 512, 128, 128
RB = 16
G, R = 4, 32
D = C // G
HB = RB // 2
HBM, VMEM = pltpu.HBM, pltpu.VMEM
VMEM_LIMIT = 32 * 1024 * 1024
WHOLE_VMEM = 60 * 1024 * 1024
MOST_VMEM = 51 * 1024 * 1024

PK_PROJ, PK_OUT, PK_NORM, PK = 0, 128, 192, 208


def dot(a, b, ca=1, cb=0):
    return lax.dot_general(a, b, (((ca,), (cb,)), ((), ())), preferred_element_type=F32)


def column(row):
    return jnp.broadcast_to(row, (C, C)).T


def norm_cols(v, gain, bias):
    mean = jnp.mean(v, 0, keepdims=True)
    cent = v - mean
    var = jnp.mean(cent * cent, 0, keepdims=True)
    return cent * lax.rsqrt(var + 1e-05) * gain + bias


def sigmoid(v):
    return 0.5 * jnp.tanh(0.5 * v) + 0.5


def gated(gate, value, half_mask):
    return (jnp.tanh(0.5 * gate) + 1.0) * (value * half_mask)


def project0_kernel(
    pair, mask, in_gain, in_bias, w, out,
    rows, mask_v, mask_s, gb, w_v, left_s, right_s, zn_s, stage, sems,
):
    small = [(in_gain, gb.at[0]), (in_bias, gb.at[1]), (w.at[0], w_v), (mask, mask_v), (mask, mask_s)]
    big = [(pair.at[:, pl.ds(T * h, T)], rows.at[h]) for h in range(G)]
    copies = [pltpu.make_async_copy(*ends, sems.at[k]) for k, ends in enumerate(small + big)]
    few = len(small)
    for copy in copies[:2] + copies[few : few + 1] + copies[2:few] + copies[few + 1 :]:
        copy.start()
    for copy in copies[:2]:
        copy.wait()
    gain, bias = column(gb[0, 0:1, :]), column(gb[1, 0:1, :])
    row0 = lax.axis_index("row") * RB
    cols = None
    for h in range(G + 1):
        if h < G:
            copies[few + h].wait()
        if h == 1:
            for copy in copies[2:few]:
                copy.wait()
            cols = mask_v[...].astype(F32) * 0.5
        for i in range(0, RB, 2):
            if h < G:
                for k in (0, 1):
                    zn_s[h, i + k] = norm_cols(rows[h, i + k].T, gain, bias).astype(BF16)
            if h > 0:
                e = h - 1
                proj = dot(w_v[...], jnp.concatenate([zn_s[e, i], zn_s[e, i + 1]], 1))
                for k in (0, 1):
                    half = cols[:, T * e : T * e + T] * mask_s[0, row0 + i + k].astype(F32)
                    part = proj[:, T * k : T * k + T]
                    left_s[e, pl.ds(i + k, D, stride=RB), :] = gated(part[0:D], part[D : 2 * D], half)
                    right_s[e, pl.ds(i + k, D, stride=RB), :] = gated(part[2 * D : 3 * D], part[3 * D :], half)
        if h > 0:
            stage[e, :, 0] = left_s[e].reshape(D, RB, T).astype(BF16)
            stage[e, :, 1] = right_s[e].reshape(D, RB, T).astype(BF16)
            copies.append(
                pltpu.make_async_copy(stage.at[e], out.at[:, :, :, pl.ds(T * e, T)], sems.at[few + G + e])
            )
            copies[-1].start()
    for copy in copies[few + G :]:
        copy.wait()


def gate0_kernel(
    pair, mask, in_gain, in_bias, w_gate, w, w_out, out_gain, out_bias, state, gate, half, own, block, mask_v, mask_s, sems
):
    at = pl.multiple_of(lax.axis_index("ch") * T, T)
    copies = [
        pltpu.make_async_copy(pair.at[:, pl.ds(at, T), :], block, sems.at[0]),
        pltpu.make_async_copy(mask.at[:, pl.ds(at, T)], mask_v, sems.at[1]),
        pltpu.make_async_copy(mask, mask_s, sems.at[2]),
    ]
    for copy in copies:
        copy.start()
    own[:PK_OUT] = w[1]
    own[PK_OUT:PK_NORM] = w_out[...].reshape(2 * D, C)
    norms = jnp.concatenate([out_gain[...], out_bias[...]], 0)
    hi = norms.astype(BF16).astype(F32)
    mid = (norms - hi).astype(BF16).astype(F32)
    low = norms - hi - mid
    tile = jnp.concatenate([hi, mid, low, jnp.zeros_like(hi)], 0)
    own[PK_NORM:] = jnp.concatenate([tile, jnp.zeros((16, C - D), F32)], 1).astype(BF16)
    gain, bias = column(in_gain[0:1, :]), column(in_bias[0:1, :])
    w_g = w_gate[0].astype(F32).T.astype(BF16)
    for copy in copies:
        copy.wait()
    row0 = lax.axis_index("row") * RB
    for i in range(RB):
        half[i : i + 1, :] = mask_v[...].astype(F32) * (0.5 * mask_s[0, row0 + i].astype(F32))
        z = block[i].T
        state[i] = z
        gate[i] = sigmoid(dot(w_g, norm_cols(z, gain, bias).astype(BF16)))


def weights_kernel(own, up, down, far, in_gain, in_bias, w, norms, pk):
    g = lax.axis_index("ch")
    pk[g] = own[...]
    pk[lax.rem(g + 3, G)] = up[...]
    pk[lax.rem(g + 1, G)] = down[...]
    pk[lax.rem(g + 2, G)] = far[...]
    for k in range(G):
        w[k] = pk[k, PK_PROJ : PK_PROJ + C]
    for k in range(G):
        parts = pk[k, PK_NORM:].astype(F32)
        parts = parts[0:4] + parts[4:8] + parts[8:12]
        for j in range(4):
            norms[j, D * k : D * k + D] = column(parts[j : j + 1])[:D]
    for layer in range(2):
        rows = jnp.concatenate(
            [pk[k, PK_OUT + D * layer : PK_OUT + D * (layer + 1)] for k in range(G)], 0
        )
        w[G + layer] = rows.astype(F32).T.astype(BF16)
    norms[4] = column(in_gain[1:2, :])
    norms[5] = column(in_bias[1:2, :])


def outgoing_kernel(a, _w, _gate, out):
    left = a[:, 0].reshape(N, N)
    for h in range(0, G, 4):
        right = a[8 * h : 8 * (h + 4), 1].reshape(T * 4, N)
        x = dot(left, right, 1, 1)
        for k in range(4):
            out[h + k] = x[:, T * k : T * k + T].reshape(R, RB, T).astype(BF16)


def incoming_kernel(b, out):
    def columns(part, h, n):
        return jnp.concatenate([b[R * k : R * k + R, part].reshape(N, T) for k in range(h, h + n)], 1)

    left = columns(0, 0, G)
    for h in range(0, G, 4):
        x = dot(left, columns(1, h, 4), 0, 0)
        for k in range(4):
            out[h + k] = x[:, T * k : T * k + T].reshape(R, RB, T).astype(BF16)


def middle_kernel(
    y, z0, gate, half_mask, w, norms, state, normed, out, ys, left_s, right_s, hid
):
    ys[...] = y[...].astype(F32).reshape(C * RB, T)
    for i in range(RB):
        hid[i] = norm_cols(ys[pl.ds(i, C, stride=RB), :], norms[0], norms[2]).astype(BF16)
    for i in range(RB):
        z = z0[i] + gate[i] * dot(w[G], hid[i])
        state[i] = z
        normed[i] = norm_cols(z, norms[4], norms[5]).astype(BF16)
    for g in range(G):
        for i in range(0, RB, 2):
            half = jnp.concatenate([half_mask[i : i + 1, :], half_mask[i + 1 : i + 2, :]], 1)
            proj = dot(w[g], jnp.concatenate([normed[i], normed[i + 1]], 1))
            left = gated(proj[0:D], proj[D : 2 * D], half)
            right = gated(proj[2 * D : 3 * D], proj[3 * D :], half)
            for k in (0, 1):
                rows = pl.ds(i + k + g * D * RB, D, stride=RB)
                left_s[rows, :] = left[:, T * k : T * k + T]
                right_s[rows, :] = right[:, T * k : T * k + T]
    out[:, 0] = left_s[...].reshape(C, RB, T).astype(BF16)
    out[:, 1] = right_s[...].reshape(C, RB, T).astype(BF16)


def last_kernel(y, state, normed, w_gate, w, norms, out0, out1, ys):
    w_g = w_gate[1].astype(F32).T.astype(BF16)
    ys[...] = y[...].astype(F32).reshape(C * RB, T)
    for i in range(RB):
        hidden = norm_cols(ys[pl.ds(i, C, stride=RB), :], norms[1], norms[3]).astype(BF16)
        gate = sigmoid(dot(w_g, normed[i]))
        z = state[i] + gate * dot(w[G + 1], hidden)
        out = (out0, out1)[i // HB]
        out[i % HB] = z.T.astype(BF16)


def spread_near_kernel(own0, own1, up0, up1, down0, down1, out, buf, sems):
    g = lax.axis_index("ch")
    copies = []
    for k, (shift, lo, hi) in enumerate([(0, own0, own1), (3, up0, up1), (1, down0, down1)]):
        buf[k, :HB] = lo[...].astype(F32)
        buf[k, HB:] = hi[...].astype(F32)
        at = pl.multiple_of(lax.rem(g + shift, G) * T, T)
        copies.append(pltpu.make_async_copy(buf.at[k], out.at[:, pl.ds(at, T), :], sems.at[k]))
        copies[-1].start()
    for copy in copies:
        copy.wait()


def spread_far_kernel(row, far, _, out, buf, sem):
    at = pl.multiple_of(lax.rem(lax.axis_index("ch") + 2, G) * T, T)
    buf[...] = far[...].astype(F32)
    copy = pltpu.make_async_copy(buf, out.at[pl.ds(row, HB), pl.ds(at, T), :], sem)
    copy.start()
    copy.wait()


def params(limit=VMEM_LIMIT):
    return pltpu.CompilerParams(vmem_limit_bytes=limit)


def call(kernel, name, outs, scratch, ins, limit=VMEM_LIMIT, out_space=None):
    return pl.pallas_call(
        kernel,
        out_shape=outs,
        in_specs=[pl.BlockSpec(memory_space=space) for _, space in ins],
        out_specs=jax.tree.map(lambda _: pl.BlockSpec(memory_space=out_space or VMEM), outs),
        scratch_shapes=scratch,
        compiler_params=params(limit),
        name=name,
    )(*[value for value, _ in ins])


def on_device(pair, mask, in_gain, in_bias, w_proj, w_gate, out_gain, out_bias, w_out):
    arr = jax.ShapeDtypeStruct
    mask = mask[None]
    w_t = jnp.transpose(w_proj, (0, 2, 3, 1)).reshape(2, 4 * D, C)
    dma = pltpu.SemaphoreType.DMA

    a = call(
        project0_kernel,
        "project0",
        arr((D, 2, RB, N), BF16),
        [
            pltpu.VMEM((G, RB, T, C), F32),
            pltpu.VMEM((1, N), jnp.int32),
            pltpu.SMEM((1, N), jnp.int32),
            pltpu.VMEM((2, 2, C), F32),
            pltpu.VMEM((4 * D, C), BF16),
            pltpu.VMEM((G, D * RB, T), F32),
            pltpu.VMEM((G, D * RB, T), F32),
            pltpu.VMEM((G, RB, C, T), BF16),
            pltpu.VMEM((G, D, 2, RB, T), BF16),
            dma((5 + 2 * G,)),
        ],
        [(v, HBM) for v in (pair, mask, in_gain, in_bias, w_t)],
        WHOLE_VMEM,
        HBM,
    )

    up = functools.partial(lax.ppermute, axis_name="ch", perm=[(k, (k + 1) % G) for k in range(G)])
    down = functools.partial(lax.ppermute, axis_name="ch", perm=[(k, (k - 1) % G) for k in range(G)])
    cross = functools.partial(lax.ppermute, axis_name="ch", perm=[(k, (k + 2) % G) for k in range(G)])

    sent = lax.all_to_all(a, "row", 0, 0)
    state, gate, half_mask, own = call(
        gate0_kernel,
        "gate0",
        (arr((RB, C, T), F32), arr((RB, C, T), F32), arr((RB, T), F32), arr((PK, C), BF16)),
        [
            pltpu.VMEM((RB, T, C), F32),
            pltpu.VMEM((1, T), jnp.int32),
            pltpu.SMEM((1, N), jnp.int32),
            dma((3,)),
        ],
        [(pair, HBM), (mask, HBM)]
        + [(v, VMEM) for v in (in_gain, in_bias, w_gate, w_t, w_out, out_gain, out_bias)],
        MOST_VMEM,
    )
    w, norms = call(
        weights_kernel,
        "weights",
        (arr((G + 2, C, C), BF16), arr((6, C, T), F32)),
        [pltpu.VMEM((G, PK, C), BF16)],
        [(v, VMEM) for v in (own, up(own), down(own), cross(own), in_gain, in_bias)],
    )
    x = call(
        outgoing_kernel,
        "outgoing",
        arr((G, R, RB, T), BF16),
        [],
        [(sent, VMEM)] + [(v, pl.ANY) for v in (w, gate)],
    )
    y = lax.all_to_all(x.reshape(G * R, RB, T), ("ch", "row"), 0, 0)
    state, normed, b = call(
        middle_kernel,
        "middle",
        (arr((RB, C, T), F32), arr((RB, C, T), BF16), arr((C, 2, RB, T), BF16)),
        [pltpu.VMEM((C * RB, T), F32)] * 3 + [pltpu.VMEM((RB, C, T), BF16)],
        [(v, VMEM) for v in (y, state, gate, half_mask, w, norms)],
    )
    b = lax.all_to_all(b, ("ch", "row"), 0, 0)
    x = call(incoming_kernel, "incoming", arr((G, R, RB, T), BF16), [], [(b, VMEM)])
    y = lax.all_to_all(x.reshape(G * R, RB, T), ("ch", "row"), 0, 0)
    half = arr((HB, T, C), BF16)
    z0, z1 = call(
        last_kernel,
        "last",
        (half, half),
        [pltpu.VMEM((C * RB, T), F32)],
        [(v, VMEM) for v in (y, state, normed, w_gate, w, norms)],
    )
    up0, down1 = up(z0), down(z1)
    up1, down0 = up(z1), down(z0)
    far0, far1 = up(up0), down(down1)
    whole = arr((RB, N, C), F32)
    near = pl.pallas_call(
        spread_near_kernel,
        out_shape=whole,
        in_specs=[pl.BlockSpec(memory_space=VMEM)] * 6,
        out_specs=pl.BlockSpec(memory_space=HBM),
        scratch_shapes=[pltpu.VMEM((3, RB, T, C), F32), dma((3,))],
        compiler_params=params(),
        name="spread_near",
    )(z0, z1, up0, up1, down0, down1)
    for row, far in ((0, far0), (HB, far1)):
        near = pl.pallas_call(
            functools.partial(spread_far_kernel, row),
            out_shape=whole,
            in_specs=[pl.BlockSpec(memory_space=VMEM), pl.BlockSpec(memory_space=HBM)],
            out_specs=pl.BlockSpec(memory_space=HBM),
            scratch_shapes=[pltpu.VMEM((HB, T, C), F32), dma],
            input_output_aliases={1: 0},
            compiler_params=params(),
            name="spread_far",
        )(far, near)
    return near


def solution(mesh):
    placed = (
        P("row", None, None),
        P(),
        P(),
        P(),
        P(None, None, None, "ch"),
        P(),
        P(None, "ch"),
        P(None, "ch"),
        P(None, "ch", None),
    )
    return jax.shard_map(
        on_device, mesh=mesh, in_specs=placed, out_specs=P("row", None, None), check_vma=False
    )
```

```python
import functools

import jax
import jax.numpy as jnp
from jax import lax
from jax.experimental import pallas as pl
from jax.experimental.pallas import tpu as pltpu
from jax.sharding import PartitionSpec as P

F32, BF16 = jnp.float32, jnp.bfloat16
N, C, T = 512, 128, 128
RB = 16
G, R = 4, 32
D = C // G
HB = RB // 2
HBM, VMEM = pltpu.HBM, pltpu.VMEM
VMEM_LIMIT = 32 * 1024 * 1024
WHOLE_VMEM = 60 * 1024 * 1024
MOST_VMEM = 51 * 1024 * 1024

PK_PROJ, PK_OUT, PK_NORM, PK = 0, 128, 192, 208


def dot(a, b, ca=1, cb=0):
    return lax.dot_general(a, b, (((ca,), (cb,)), ((), ())), preferred_element_type=F32)


def column(row):
    return jnp.broadcast_to(row, (C, C)).T


def norm_cols(v, gain, bias):
    mean = jnp.mean(v, 0, keepdims=True)
    cent = v - mean
    var = jnp.mean(cent * cent, 0, keepdims=True)
    return cent * lax.rsqrt(var + 1e-05) * gain + bias


def sigmoid(v):
    return 0.5 * jnp.tanh(0.5 * v) + 0.5


def gated(half_gate, value, half_mask):
    return (jnp.tanh(half_gate) + 1.0) * (value * half_mask)


def halve_gates(w):
    row = lax.broadcasted_iota(jnp.int32, w.shape, 0)
    is_gate = (row < D) | ((row >= 2 * D) & (row < 3 * D))
    return jnp.where(is_gate, 0.5 * w.astype(F32), w.astype(F32)).astype(BF16)


def project0_kernel(
    pair, mask, in_gain, in_bias, w, out,
    rows, mask_v, mask_s, gb, w_v, left_s, right_s, zn_s, stage, sems,
):
    small = [(in_gain, gb.at[0]), (in_bias, gb.at[1]), (w.at[0], w_v), (mask, mask_v), (mask, mask_s)]
    big = [(pair.at[:, pl.ds(T * h, T)], rows.at[h]) for h in range(G)]
    copies = [pltpu.make_async_copy(*ends, sems.at[k]) for k, ends in enumerate(small + big)]
    few = len(small)
    for copy in copies[:2] + copies[few : few + 1] + copies[2:few] + copies[few + 1 :]:
        copy.start()
    for copy in copies[:2]:
        copy.wait()
    gain, bias = column(gb[0, 0:1, :]), column(gb[1, 0:1, :])
    row0 = lax.axis_index("row") * RB
    cols = None
    for h in range(G + 1):
        if h < G:
            copies[few + h].wait()
        if h == 1:
            for copy in copies[2:few]:
                copy.wait()
            w_v[...] = halve_gates(w_v[...])
            cols = mask_v[...].astype(F32) * 0.5
        for i in range(0, RB, 2):
            if h < G:
                for k in (0, 1):
                    zn_s[h, i + k] = norm_cols(rows[h, i + k].T, gain, bias).astype(BF16)
            if h > 0:
                e = h - 1
                proj = dot(w_v[...], jnp.concatenate([zn_s[e, i], zn_s[e, i + 1]], 1))
                for k in (0, 1):
                    half = cols[:, T * e : T * e + T] * mask_s[0, row0 + i + k].astype(F32)
                    part = proj[:, T * k : T * k + T]
                    left_s[e, pl.ds(i + k, D, stride=RB), :] = gated(part[0:D], part[D : 2 * D], half)
                    right_s[e, pl.ds(i + k, D, stride=RB), :] = gated(part[2 * D : 3 * D], part[3 * D :], half)
        if h > 0:
            stage[e, :, 0] = left_s[e].reshape(D, RB, T).astype(BF16)
            stage[e, :, 1] = right_s[e].reshape(D, RB, T).astype(BF16)
            copies.append(
                pltpu.make_async_copy(stage.at[e], out.at[:, :, :, pl.ds(T * e, T)], sems.at[few + G + e])
            )
            copies[-1].start()
    for copy in copies[few + G :]:
        copy.wait()


def gate0_kernel(
    pair, mask, in_gain, in_bias, w_gate, w, w_out, out_gain, out_bias, state, gate, half, own, block, mask_v, mask_s, sems
):
    at = pl.multiple_of(lax.axis_index("ch") * T, T)
    copies = [
        pltpu.make_async_copy(pair.at[:, pl.ds(at, T), :], block, sems.at[0]),
        pltpu.make_async_copy(mask.at[:, pl.ds(at, T)], mask_v, sems.at[1]),
        pltpu.make_async_copy(mask, mask_s, sems.at[2]),
    ]
    for copy in copies:
        copy.start()
    own[:PK_OUT] = w[1]
    own[PK_OUT:PK_NORM] = w_out[...].reshape(2 * D, C)
    norms = jnp.concatenate([out_gain[...], out_bias[...]], 0)
    hi = norms.astype(BF16).astype(F32)
    mid = (norms - hi).astype(BF16).astype(F32)
    low = norms - hi - mid
    tile = jnp.concatenate([hi, mid, low, jnp.zeros_like(hi)], 0)
    own[PK_NORM:] = jnp.concatenate([tile, jnp.zeros((16, C - D), F32)], 1).astype(BF16)
    gain, bias = column(in_gain[0:1, :]), column(in_bias[0:1, :])
    w_g = w_gate[0].astype(F32).T.astype(BF16)
    for copy in copies:
        copy.wait()
    row0 = lax.axis_index("row") * RB
    for i in range(RB):
        half[i : i + 1, :] = mask_v[...].astype(F32) * (0.5 * mask_s[0, row0 + i].astype(F32))
        z = block[i].T
        state[i] = z
        gate[i] = sigmoid(dot(w_g, norm_cols(z, gain, bias).astype(BF16)))


def weights_kernel(own, up, down, far, in_gain, in_bias, w_gate, w, norms, pk):
    g = lax.axis_index("ch")
    pk[g] = own[...]
    pk[lax.rem(g + 3, G)] = up[...]
    pk[lax.rem(g + 1, G)] = down[...]
    pk[lax.rem(g + 2, G)] = far[...]
    for k in range(G):
        w[k] = halve_gates(pk[k, PK_PROJ : PK_PROJ + C])
    for k in range(G):
        parts = pk[k, PK_NORM:].astype(F32)
        parts = parts[0:4] + parts[4:8] + parts[8:12]
        for j in range(4):
            norms[j, D * k : D * k + D] = column(parts[j : j + 1])[:D]
    for layer in range(2):
        rows = jnp.concatenate(
            [pk[k, PK_OUT + D * layer : PK_OUT + D * (layer + 1)] for k in range(G)], 0
        )
        w[G + layer] = (rows.astype(F32).T * (1.0, 0.5)[layer]).astype(BF16)
    w[G + 2] = (0.5 * w_gate[1].astype(F32).T).astype(BF16)
    norms[4] = column(in_gain[1:2, :])
    norms[5] = column(in_bias[1:2, :])


def outgoing_kernel(a, _w, _gate, _state, _norms, _half, out):
    left = a[:, 0].reshape(N, N)
    for h in range(0, G, 4):
        right = a[8 * h : 8 * (h + 4), 1].reshape(T * 4, N)
        x = dot(left, right, 1, 1)
        for k in range(4):
            out[h + k] = x[:, T * k : T * k + T].reshape(R, RB, T).astype(BF16)


def incoming_kernel(b, out):
    def columns(part, h, n):
        return jnp.concatenate([b[R * k : R * k + R, part].reshape(N, T) for k in range(h, h + n)], 1)

    left = columns(0, 0, G)
    for h in range(0, G, 4):
        x = dot(left, columns(1, h, 4), 0, 0)
        for k in range(4):
            out[h + k] = x[:, T * k : T * k + T].reshape(R, RB, T).astype(BF16)


def middle_kernel(
    y, z0, gate, half_mask, w, norms, state, normed, out, ys, left_s, right_s, hid
):
    ys[...] = y[...].astype(F32).reshape(C * RB, T)
    for i in range(RB):
        hid[i] = norm_cols(ys[pl.ds(i, C, stride=RB), :], norms[0], norms[2]).astype(BF16)
    for i in range(RB):
        z = z0[i] + gate[i] * dot(w[G], hid[i])
        state[i] = z
        normed[i] = norm_cols(z, norms[4], norms[5]).astype(BF16)
    for g in range(G):
        for i in range(0, RB, 2):
            half = jnp.concatenate([half_mask[i : i + 1, :], half_mask[i + 1 : i + 2, :]], 1)
            proj = dot(w[g], jnp.concatenate([normed[i], normed[i + 1]], 1))
            left = gated(proj[0:D], proj[D : 2 * D], half)
            right = gated(proj[2 * D : 3 * D], proj[3 * D :], half)
            for k in (0, 1):
                rows = pl.ds(i + k + g * D * RB, D, stride=RB)
                left_s[rows, :] = left[:, T * k : T * k + T]
                right_s[rows, :] = right[:, T * k : T * k + T]
    out[:, 0] = left_s[...].reshape(C, RB, T).astype(BF16)
    out[:, 1] = right_s[...].reshape(C, RB, T).astype(BF16)


def last_kernel(y, state, normed, w, norms, out0, out1, ys):
    ys[...] = y[...].astype(F32).reshape(C * RB, T)
    for i in range(RB):
        hidden = norm_cols(ys[pl.ds(i, C, stride=RB), :], norms[1], norms[3]).astype(BF16)
        twice_gate = jnp.tanh(dot(w[G + 2], normed[i])) + 1.0
        z = state[i] + twice_gate * dot(w[G + 1], hidden)
        out = (out0, out1)[i // HB]
        out[i % HB] = z.T.astype(BF16)


def spread_near_kernel(own0, own1, up0, up1, down0, down1, out, buf, sems):
    g = lax.axis_index("ch")
    copies = []
    for k, (shift, lo, hi) in enumerate([(0, own0, own1), (3, up0, up1), (1, down0, down1)]):
        buf[k, :HB] = lo[...].astype(F32)
        buf[k, HB:] = hi[...].astype(F32)
        at = pl.multiple_of(lax.rem(g + shift, G) * T, T)
        copies.append(pltpu.make_async_copy(buf.at[k], out.at[:, pl.ds(at, T), :], sems.at[k]))
        copies[-1].start()
    for copy in copies:
        copy.wait()


def spread_far_kernel(far0, far1, _, out, buf, sems):
    at = pl.multiple_of(lax.rem(lax.axis_index("ch") + 2, G) * T, T)
    copies = []
    for k, far in enumerate((far0, far1)):
        buf[k] = far[...].astype(F32)
        copies.append(
            pltpu.make_async_copy(buf.at[k], out.at[pl.ds(k * HB, HB), pl.ds(at, T), :], sems.at[k])
        )
        copies[-1].start()
    for copy in copies:
        copy.wait()


def params(limit=VMEM_LIMIT):
    return pltpu.CompilerParams(vmem_limit_bytes=limit)


def call(kernel, name, outs, scratch, ins, limit=VMEM_LIMIT, out_space=None):
    return pl.pallas_call(
        kernel,
        out_shape=outs,
        in_specs=[pl.BlockSpec(memory_space=space) for _, space in ins],
        out_specs=jax.tree.map(lambda _: pl.BlockSpec(memory_space=out_space or VMEM), outs),
        scratch_shapes=scratch,
        compiler_params=params(limit),
        name=name,
    )(*[value for value, _ in ins])


def on_device(pair, mask, in_gain, in_bias, w_proj, w_gate, out_gain, out_bias, w_out):
    arr = jax.ShapeDtypeStruct
    mask = mask[None]
    w_t = jnp.transpose(w_proj, (0, 2, 3, 1)).reshape(2, 4 * D, C)
    dma = pltpu.SemaphoreType.DMA

    a = call(
        project0_kernel,
        "project0",
        arr((D, 2, RB, N), BF16),
        [
            pltpu.VMEM((G, RB, T, C), F32),
            pltpu.VMEM((1, N), jnp.int32),
            pltpu.SMEM((1, N), jnp.int32),
            pltpu.VMEM((2, 2, C), F32),
            pltpu.VMEM((4 * D, C), BF16),
            pltpu.VMEM((G, D * RB, T), F32),
            pltpu.VMEM((G, D * RB, T), F32),
            pltpu.VMEM((G, RB, C, T), BF16),
            pltpu.VMEM((G, D, 2, RB, T), BF16),
            dma((5 + 2 * G,)),
        ],
        [(v, HBM) for v in (pair, mask, in_gain, in_bias, w_t)],
        WHOLE_VMEM,
        HBM,
    )

    up = functools.partial(lax.ppermute, axis_name="ch", perm=[(k, (k + 1) % G) for k in range(G)])
    down = functools.partial(lax.ppermute, axis_name="ch", perm=[(k, (k - 1) % G) for k in range(G)])
    cross = functools.partial(lax.ppermute, axis_name="ch", perm=[(k, (k + 2) % G) for k in range(G)])

    sent = lax.all_to_all(a, "row", 0, 0)
    state, gate, half_mask, own = call(
        gate0_kernel,
        "gate0",
        (arr((RB, C, T), F32), arr((RB, C, T), F32), arr((RB, T), F32), arr((PK, C), BF16)),
        [
            pltpu.VMEM((RB, T, C), F32),
            pltpu.VMEM((1, T), jnp.int32),
            pltpu.SMEM((1, N), jnp.int32),
            dma((3,)),
        ],
        [(pair, HBM), (mask, HBM)]
        + [(v, VMEM) for v in (in_gain, in_bias, w_gate, w_t, w_out, out_gain, out_bias)],
        MOST_VMEM,
    )
    w, norms = call(
        weights_kernel,
        "weights",
        (arr((G + 3, C, C), BF16), arr((6, C, T), F32)),
        [pltpu.VMEM((G, PK, C), BF16)],
        [(v, VMEM) for v in (own, up(own), down(own), cross(own), in_gain, in_bias, w_gate)],
    )
    x = call(
        outgoing_kernel,
        "outgoing",
        arr((G, R, RB, T), BF16),
        [],
        [(sent, VMEM)] + [(v, pl.ANY) for v in (w, gate, state, norms, half_mask)],
    )
    y = lax.all_to_all(x.reshape(G * R, RB, T), ("ch", "row"), 0, 0)
    state, normed, b = call(
        middle_kernel,
        "middle",
        (arr((RB, C, T), F32), arr((RB, C, T), BF16), arr((C, 2, RB, T), BF16)),
        [pltpu.VMEM((C * RB, T), F32)] * 3 + [pltpu.VMEM((RB, C, T), BF16)],
        [(v, VMEM) for v in (y, state, gate, half_mask, w, norms)],
    )
    b = lax.all_to_all(b, ("ch", "row"), 0, 0)
    x = call(incoming_kernel, "incoming", arr((G, R, RB, T), BF16), [], [(b, VMEM)])
    y = lax.all_to_all(x.reshape(G * R, RB, T), ("ch", "row"), 0, 0)
    half = arr((HB, T, C), BF16)
    z0, z1 = call(
        last_kernel,
        "last",
        (half, half),
        [pltpu.VMEM((C * RB, T), F32)],
        [(v, VMEM) for v in (y, state, normed, w, norms)],
    )
    up0, down1 = up(z0), down(z1)
    up1, down0 = up(z1), down(z0)
    far0, far1 = up(up0), down(down1)
    whole = arr((RB, N, C), F32)
    near = pl.pallas_call(
        spread_near_kernel,
        out_shape=whole,
        in_specs=[pl.BlockSpec(memory_space=VMEM)] * 6,
        out_specs=pl.BlockSpec(memory_space=HBM),
        scratch_shapes=[pltpu.VMEM((3, RB, T, C), F32), dma((3,))],
        compiler_params=params(),
        name="spread_near",
    )(z0, z1, up0, up1, down0, down1)
    return pl.pallas_call(
        spread_far_kernel,
        out_shape=whole,
        in_specs=[pl.BlockSpec(memory_space=VMEM)] * 2 + [pl.BlockSpec(memory_space=HBM)],
        out_specs=pl.BlockSpec(memory_space=HBM),
        scratch_shapes=[pltpu.VMEM((2, HB, T, C), F32), dma((2,))],
        input_output_aliases={2: 0},
        compiler_params=params(),
        name="spread_far",
    )(far0, far1, near)


def solution(mesh):
    placed = (
        P("row", None, None),
        P(),
        P(),
        P(),
        P(None, None, None, "ch"),
        P(),
        P(None, "ch"),
        P(None, "ch"),
        P(None, "ch", None),
    )
    return jax.shard_map(
        on_device, mesh=mesh, in_specs=placed, out_specs=P("row", None, None), check_vma=False
    )
```
